512 devices in a mesh: frm: 32 (over y, z_lo), hgt: 4 (over x), wid: 4 (over z_hi, core).
Axes of the slice: x: 4, y: 8, z: 8 (z_hi: 2, z_lo: 4; z = z_hi * 4 + z_lo), core: 2. Of those that a mesh axis runs over, the one named last changes fastest.
Arguments:
- video: bfloat16 [1280, 1536, 512], P('frm', 'hgt', 'wid'), may hold values from -30 to 30
- height_factor: bfloat16 [1536, 256], P('hgt'), may hold values from -0.15625 to 0.15625
- width_factor: bfloat16 [512, 256], P('wid'), may hold values from -0.25 to 0.25
- start_basis: float32 [1280, 64], P('frm'), may hold values from -6 to 6
Outputs:
- gram: float32 [1280, 1280], P('frm', ('hgt', 'wid'))
- frame_factor: float32 [1280, 64], P('frm')
The draws below stay inside these ranges and needn't reach their ends.
All inputs are finite; a program needn't handle non-finite values.
Results may differ from the reference program's by a relative error of at most 0.02.
Values may be sent and summed in bfloat16 or wider, within the bound.
No kernel may reach another device: no remote copies, remote signals or barrier semaphores. Data moves between devices by JAX's collectives and lax.ppermute only.
A program may use at most 64 MiB of HBM per device.

```python
import math
import jax
import jax.numpy as jnp
from jax import lax

RANK_H = 256
RANK_W = 256
RANK_F = 64
FRM_DEV = 40
HGT_DEV = 384
WID_DEV = 128
ITERS = 3
FRAMES = 1280
HEIGHT = 1536
WIDTH = 512
N_HGT = 4
N_WID = 4


def draw_video(key, part):
    key = jax.random.fold_in(key, 7)
    noise_key, bright_key, scene_key, weight_key = jax.random.split(key, 4)
    shape = (FRAMES, HEIGHT, WIDTH)
    base = jax.random.truncated_normal(noise_key, -4.0, 4.0, shape, jnp.float32)
    mixing = 0.6
    bright = jnp.exp(jax.random.uniform(bright_key, (FRAMES, 1, 1), jnp.float32, 0.0, math.log(3.0)))
    scene = jax.random.truncated_normal(scene_key, -4.0, 4.0, (1, HEIGHT, WIDTH), jnp.float32)
    weights = jax.random.uniform(weight_key, (FRAMES, 1, 1), jnp.float32, -1.0, 1.0)
    frames = bright * (base + mixing * jnp.roll(base, 1, axis=0)) + weights * scene
    return frames.astype(jnp.bfloat16)


def levels(rng, shape, shards, low, largest):
    factor_of, own = 1.0, jax.random.fold_in(rng, 6)
    for axis_at, blocks in shards:
        draws = jnp.exp(jax.random.uniform(jax.random.fold_in(own, axis_at), (blocks,), jnp.float32, low / len(shards), largest / len(shards)))
        factor_of = factor_of * jnp.repeat(draws, shape[axis_at] // blocks).reshape([-1 if axis == axis_at else 1 for axis in range(len(shape))])
    return factor_of


def noise(rng, extent, deviation, limit, pieces=(), dtype=jnp.bfloat16):
    factor_of = levels(rng, extent, pieces, -0.22, 0.18) if pieces else 1.0
    array = jax.random.normal(rng, extent, jnp.float32) * deviation * factor_of
    return jnp.minimum(jnp.maximum(array, -limit), limit).astype(dtype)


def setup_inputs(seed: int = 0) -> dict:
    key_of = jax.random.split(jax.random.key(seed), 5)
    return {
        "video": draw_video(jax.random.fold_in(key_of[4], 71), 0),
        "height_factor": noise(key_of[1], (HEIGHT, RANK_H), HEIGHT ** -0.5, 0.15625, ((0, 4),)),
        "width_factor": noise(key_of[2], (WIDTH, RANK_W), WIDTH ** -0.5, 0.25, ((0, 4),)),
        "start_basis": noise(key_of[3], (FRAMES, RANK_F), 1.0, 6.0, ((0, 32),), jnp.float32),
    }


def project_block(block, height_factor, width_factor):
    rows = block.astype(jnp.float32).reshape(FRM_DEV, N_HGT, HGT_DEV, WIDTH)
    hfac = height_factor.astype(jnp.float32).reshape(N_HGT, HGT_DEV, RANK_H)
    parts = jnp.einsum('fkhw,khr->krfw', rows, hfac).astype(jnp.bfloat16)
    mid = lax.optimization_barrier(jnp.sum(parts.astype(jnp.float32), axis=0)).astype(jnp.bfloat16)
    cols = mid.astype(jnp.float32).reshape(RANK_H, FRM_DEV, N_WID, WID_DEV)
    wfac = width_factor.astype(jnp.float32).reshape(N_WID, WID_DEV, RANK_W)
    second = jnp.einsum('afkw,kwb->kfab', cols, wfac).astype(jnp.bfloat16)
    return lax.optimization_barrier(jnp.sum(second.astype(jnp.float32), axis=0)).astype(jnp.bfloat16)

def reference(video, height_factor, width_factor, start_basis):
    frames = video.shape[0]
    blocks = video.reshape(frames // FRM_DEV, FRM_DEV, HEIGHT, WIDTH)
    core = lax.map(lambda block: project_block(block, height_factor, width_factor), blocks)
    flat = core.reshape(frames, RANK_H * RANK_W)
    gram = jnp.dot(flat.astype(jnp.float32), flat.T.astype(jnp.float32), preferred_element_type=jnp.float32) / float(RANK_H * RANK_W)
    basis = start_basis
    for step in range(ITERS):
        product = jnp.dot(gram, basis, precision=lax.Precision.HIGHEST)
        small = jnp.dot(product.T, product, precision=lax.Precision.HIGHEST)
        lower = jnp.linalg.cholesky(small)
        basis = lax.linalg.triangular_solve(lower, product, left_side=False, lower=True, transpose_a=True)
    return (gram, basis * math.sqrt(frames))
```

```python
import math

import jax
import jax.numpy as jnp
from jax import lax
from jax.experimental import pallas as pl
from jax.experimental.pallas import tpu as pltpu
from jax.sharding import Mesh, PartitionSpec as P

ITERS = 3
Z_HI = 2
CORES = 2
Z_LO = 4
ALL = ("y", "zl", "x", "zh", "c")


def mid_kernel(video_ref, factor_ref, out_ref, acc):
    frames, _, _ = video_ref.shape
    rank = factor_ref.shape[0]

    @pl.loop(0, frames)
    def _(f):
        acc[pl.ds(pl.multiple_of(f * rank, rank), rank), :] = jnp.dot(
            factor_ref[...], video_ref[f], preferred_element_type=jnp.float32
        )

    @pl.loop(0, rank)
    def _(r):
        out_ref[r] = acc[pl.ds(r, frames, stride=rank), :].astype(out_ref.dtype)


def mid_partial(video, factor_t):
    frames, rows, cols = video.shape
    rank = factor_t.shape[0]
    return pl.pallas_call(
        mid_kernel,
        out_shape=jax.ShapeDtypeStruct((rank, frames, cols), jnp.bfloat16),
        in_specs=[pl.BlockSpec(memory_space=pltpu.VMEM)] * 2,
        out_specs=pl.BlockSpec(memory_space=pltpu.VMEM),
        scratch_shapes=[pltpu.VMEM((frames * rank, cols), jnp.float32)],
        compiler_params=pltpu.CompilerParams(vmem_limit_bytes=40 << 20),
        cost_estimate=pl.CostEstimate(
            flops=2 * frames * rows * cols * rank,
            bytes_accessed=2 * (frames * cols * (rows + rank) + rank * rows),
            transcendentals=0,
        ),
        name="mid_partial",
    )(video, factor_t)


def local(video, height_factor, width_factor, start_basis):
    rank_h = height_factor.shape[1]
    rank_w = width_factor.shape[1]
    frames_dev, _, cols = video.shape
    frm = lax.axis_index(("y", "zl"))
    core_at = lax.axis_index("c")
    total = frames_dev * lax.axis_size(("y", "zl"))

    width_pair = lax.all_gather(width_factor, "zh", axis=0)
    mid = mid_partial(video, height_factor.T)
    mid = lax.psum_scatter(mid, "x", scatter_dimension=0, tiled=True)

    mid = lax.all_to_all(mid, ("zh", "y", "zl"), 0, 0, tiled=True)
    mid = mid.reshape(Z_HI, total, cols)
    part = jnp.einsum("kfw,kws->fs", mid, width_pair, preferred_element_type=jnp.float32)
    half = rank_w // CORES
    low, high = part[:, :half], part[:, half:]
    first = core_at == 0
    sent = jnp.where(first, high, low).astype(jnp.bfloat16)
    came = lax.ppermute(sent, "c", [(0, 1), (1, 0)])
    kept = jnp.where(first, low, high).astype(jnp.bfloat16)
    core = (kept.astype(jnp.float32) + came.astype(jnp.float32)).astype(jnp.bfloat16)

    gram = lax.dot_general(core, core, (((1,), (1,)), ((), ())), preferred_element_type=jnp.float32)
    gram = gram / float(rank_h * rank_w)

    place = (lax.axis_index("x") == 0) & (lax.axis_index("zh") == 0) & first
    shard = jnp.where(place, start_basis, 0.0).T
    basis_t = lax.dynamic_update_slice(
        jnp.zeros((shard.shape[0], total), jnp.float32), shard, (0, frm * frames_dev)
    )
    both = lax.psum(jnp.concatenate([gram, basis_t], axis=0), ALL)
    gram, basis = both[:total], both[total:].T

    group = lax.axis_index(("x", "zh", "c"))
    block = total // lax.axis_size(("x", "zh", "c"))
    gram_out = lax.dynamic_slice(gram, (frm * frames_dev, group * block), (frames_dev, block))

    for _ in range(ITERS):
        product = jnp.dot(gram, basis, precision=lax.Precision.HIGHEST)
        small = jnp.dot(product.T, product, precision=lax.Precision.HIGHEST)
        lower = jnp.linalg.cholesky(small)
        basis = lax.linalg.triangular_solve(
            lower, product, left_side=False, lower=True, transpose_a=True
        )
    mine = lax.dynamic_slice_in_dim(basis, frm * frames_dev, frames_dev, 0)
    return (gram_out, mine * math.sqrt(total))


def solution(mesh):
    frm, hgt, _ = mesh.devices.shape
    fine = Mesh(
        mesh.devices.reshape(frm // Z_LO, Z_LO, hgt, Z_HI, CORES), ("y", "zl", "x", "zh", "c")
    )
    frm, hgt, wid = ("y", "zl"), "x", ("zh", "c")
    return jax.shard_map(
        local,
        mesh=fine,
        in_specs=(P(frm, hgt, wid), P(hgt, None), P(wid, None), P(frm, None)),
        out_specs=(P(frm, ("x", "zh", "c")), P(frm, None)),
        check_vma=False,
    )
```

```python
import math

import jax
import jax.numpy as jnp
from jax import lax
from jax.experimental import pallas as pl
from jax.experimental.pallas import tpu as pltpu
from jax.sharding import Mesh, PartitionSpec as P

ITERS = 3
Z_HI = 2
CORES = 2
Z_LO = 4
N_X = 4
LANES = 128
PLANE = ("zh", "y", "zl")
VMEM = pl.BlockSpec(memory_space=pltpu.VMEM)
SMEM = pl.BlockSpec(memory_space=pltpu.SMEM)
PARAMS = pltpu.CompilerParams(vmem_limit_bytes=40 << 20)
F32 = jnp.float32
HIGHEST = lax.Precision.HIGHEST


def shape(*dims, dtype=F32):
    return jax.ShapeDtypeStruct(dims, dtype)


def gram_kernel(scale, at, own, left, right, far_a, far_b, kept, sent, core, acc):
    total, depth = own.shape
    strip = kept.shape[1]
    core[:, 0:depth] = own[...]
    core[:, depth : 2 * depth] = left[...]
    core[:, 2 * depth : 3 * depth] = right[...]
    core[0 : total // 2, 3 * depth :] = far_a[...]
    core[total // 2 :, 3 * depth :] = far_b[...]
    rows_x = total // N_X
    rows = core[pl.ds(pl.multiple_of(at[0] * rows_x, 64), rows_x), :]
    mine = at[1]
    wide = 2 * LANES
    for pair in range(total // wide):
        acc[...] = scale * lax.dot_general(
            rows,
            core[pair * wide : (pair + 1) * wide, :],
            (((1,), (1,)), ((), ())),
            preferred_element_type=F32,
        )
        for side in range(2):
            tile = 2 * pair + side
            lanes = slice(side * LANES, (side + 1) * LANES)
            for zh in range(Z_HI):
                base = zh * CORES * strip
                keep_at = pl.multiple_of(base + mine * strip, 8)
                send_at = pl.multiple_of(base + (1 - mine) * strip, 8)
                kept[tile * Z_HI + zh] = acc[pl.ds(keep_at, strip), lanes]
                sent[tile * Z_HI + zh] = acc[pl.ds(send_at, strip), lanes]


def pack_kernel(a, b, out):
    pieces, rows, _ = out.shape
    for j in range(pieces):
        out[j] = a[j * rows : (j + 1) * rows, :] + b[j * rows : (j + 1) * rows, :]


def sum_kernel(parts, out):
    total = jnp.sum(parts[...], axis=0)
    out[...] = jnp.broadcast_to(total[None], out.shape)


def packed_product(gram, basis):
    product = jnp.dot(gram, basis, precision=HIGHEST, preferred_element_type=F32)
    strip = product.shape[0] // Z_HI
    return jnp.concatenate([product[:strip], product[strip:]], axis=1)


def first_kernel(pieces, basis, gram, out, flat):
    count, rows, _ = pieces.shape
    for j in range(count):
        flat[j * rows : (j + 1) * rows, :] = pieces[j]
    mine, total = gram.shape
    for t in range(total // LANES):
        gram[:, t * LANES : (t + 1) * LANES] = flat[t * mine : (t + 1) * mine, :]
    out[...] = packed_product(gram[...], basis[...])


def unpack_product(at, four, other, full):
    rank = full.shape[1]
    strip = four.shape[1]
    for j in range(N_X):
        chip = lax.rem(at[0] + j, N_X) * (Z_HI * CORES * strip)
        for ref, core in ((four, at[1]), (other, 1 - at[1])):
            block = ref[j]
            for zh in range(Z_HI):
                start = pl.multiple_of(chip + zh * CORES * strip + core * strip, 8)
                full[pl.ds(start, strip), :] = block[:, zh * rank : (zh + 1) * rank]


def inverse_factor(small):
    n = small.shape[0]
    group = 8
    row_id = lax.broadcasted_iota(jnp.int32, (n, n), 0)
    col_id = lax.broadcasted_iota(jnp.int32, (n, n), 1)
    eye = (row_id == col_id).astype(F32)
    whole = jnp.concatenate([small, eye], axis=1)
    blocks = [whole[g * group : (g + 1) * group] for g in range(n // group)]
    sub = lax.broadcasted_iota(jnp.int32, (group, 1), 0)
    scaled = []
    for k in range(n):
        g, i = divmod(k, group)
        row = blocks[g][i : i + 1, :]
        pivot = row[:, k : k + 1]
        row = row * (1.0 / pivot)
        for b in range(g, n // group):
            col = blocks[b][:, k : k + 1]
            if b == g:
                col = jnp.where(sub > i, col, 0.0)
            blocks[b] = blocks[b] - col * row
    whole = jnp.concatenate(blocks, axis=0)
    diag = jnp.sum(whole[:, :n] * eye, axis=1, keepdims=True)
    return whole[:, n:] * (1.0 / jnp.sqrt(diag))


def factor_of(full):
    small = lax.dot_general(
        full, full, (((0,), (0,)), ((), ())), precision=HIGHEST, preferred_element_type=F32
    )
    return inverse_factor(small)


def apply_factor(rows, inverse):
    return lax.dot_general(
        rows, inverse, (((1,), (1,)), ((), ())), precision=HIGHEST, preferred_element_type=F32
    )


def step_kernel(at, four, other, gram, out, full):
    unpack_product(at, four, other, full)
    product = full[...]
    basis = apply_factor(product, factor_of(product))
    out[...] = packed_product(gram[...], basis)


def last_kernel(at, four, other, out, full):
    unpack_product(at, four, other, full)
    inverse = factor_of(full[...])
    frames = out.shape[0]
    rows = full[pl.ds(pl.multiple_of(at[2] * frames, 8), frames), :]
    out[...] = apply_factor(rows, inverse) * math.sqrt(full.shape[0])


def call(kernel, outs, ins, args, scratch=()):
    return pl.pallas_call(
        kernel,
        out_shape=outs,
        in_specs=ins,
        out_specs=jax.tree.map(lambda _: VMEM, outs),
        scratch_shapes=list(scratch),
        compiler_params=PARAMS,
    )(*args)


def shift(x, by):
    return lax.ppermute(x, "x", [(i, (i + by) % N_X) for i in range(N_X)])


def swap(x, axis):
    return lax.ppermute(x, axis, [(0, 1), (1, 0)])


def local(video, height_factor, width_factor, start_basis):
    rank_h = height_factor.shape[1]
    rank_w = width_factor.shape[1]
    rank_f = start_basis.shape[1]
    frames_dev, _, cols = video.shape
    frm = lax.axis_index(("y", "zl"))
    frm_count = lax.axis_size(("y", "zl"))
    total = frames_dev * frm_count
    x_at, zh_at, core_at = lax.axis_index("x"), lax.axis_index("zh"), lax.axis_index("c")
    first = core_at == 0
    at = jnp.stack([x_at, core_at, frm]).astype(jnp.int32)

    mid = jnp.einsum(
        "fhw,hr->rfw", video, height_factor, preferred_element_type=F32
    ).astype(jnp.bfloat16)
    mid, width, start = lax.optimization_barrier((mid, width_factor, start_basis))
    mid = lax.psum_scatter(mid, "x", scatter_dimension=0, tiled=True)
    width_other = swap(width, "zh")
    basis = lax.all_to_all(
        jnp.broadcast_to(start[None], (frm_count,) + start.shape), ("y", "zl"), 0, 0, tiled=True
    )
    mid, width_other, basis = lax.optimization_barrier((mid, width_other, basis))
    basis = basis.reshape(total, rank_f)

    mid = lax.all_to_all(mid, PLANE, 0, 0, tiled=True).reshape(Z_HI, total, cols)
    low_width = jnp.where(zh_at == 0, width, width_other)
    high_width = jnp.where(zh_at == 0, width_other, width)
    part = jnp.dot(mid[0], low_width, preferred_element_type=F32) + jnp.dot(
        mid[1], high_width, preferred_element_type=F32
    )
    half = rank_w // CORES
    low, high = part[:, :half], part[:, half:]
    came = swap(jnp.where(first, high, low).astype(jnp.bfloat16), "c")
    own = jnp.where(first, low, high).astype(jnp.bfloat16)
    core = (own.astype(F32) + came.astype(F32)).astype(jnp.bfloat16)

    left, right = shift(core, 1), shift(core, -1)
    far_a, far_b = shift(left[: total // 2], 1), shift(right[total // 2 :], -1)

    strip = total // (N_X * Z_HI * CORES)
    mine = Z_HI * strip
    tiles = total // LANES
    kept, sent = call(
        lambda *refs: gram_kernel(1.0 / (rank_h * rank_w), *refs),
        [shape(tiles * Z_HI, strip, LANES)] * 2,
        [SMEM] + [VMEM] * 5,
        (at, core, left, right, far_a, far_b),
        [
            pltpu.VMEM((total, N_X * half), jnp.bfloat16),
            pltpu.VMEM((total // N_X, 2 * LANES), F32),
        ],
    )
    came = swap(sent, "c")
    flat_rows = tiles * mine
    count = lax.axis_size(PLANE)
    pieces = call(
        pack_kernel,
        shape(count, flat_rows // count, LANES),
        [VMEM] * 2,
        (kept.reshape(flat_rows, LANES), came.reshape(flat_rows, LANES)),
    )
    pieces = lax.all_to_all(pieces, PLANE, 0, 0, tiled=True)
    pieces = call(sum_kernel, shape(*pieces.shape), [VMEM], (pieces,))
    pieces = lax.all_to_all(pieces, PLANE, 0, 0, tiled=True)

    gram, packed = call(
        first_kernel,
        [shape(mine, total), shape(strip, Z_HI * rank_f)],
        [VMEM] * 2,
        (pieces, basis),
        [pltpu.VMEM((flat_rows, LANES), F32)],
    )
    full = pltpu.VMEM((total, rank_f), F32)
    for step in range(ITERS):
        near, behind, across = shift(packed, -1), shift(packed, 1), shift(packed, 2)
        four = jnp.stack([packed, near, across, behind])
        other = swap(four, "c")
        if step < ITERS - 1:
            packed = call(
                step_kernel,
                shape(strip, Z_HI * rank_f),
                [SMEM] + [VMEM] * 3,
                (at, four, other, gram),
                [full],
            )
        else:
            factor = call(
                last_kernel,
                shape(frames_dev, rank_f),
                [SMEM] + [VMEM] * 2,
                (at, four, other),
                [full],
            )
    strip_rows = lax.dynamic_slice_in_dim(gram, zh_at * strip, strip, 0)
    gram_out = lax.dynamic_slice_in_dim(strip_rows.T, frm * frames_dev, frames_dev, 0)
    return (gram_out, factor)


def solution(mesh):
    frm, hgt, _ = mesh.devices.shape
    fine = Mesh(
        mesh.devices.reshape(frm // Z_LO, Z_LO, hgt, Z_HI, CORES), ("y", "zl", "x", "zh", "c")
    )
    frm, hgt, wid = ("y", "zl"), "x", ("zh", "c")
    return jax.shard_map(
        local,
        mesh=fine,
        in_specs=(P(frm, hgt, wid), P(hgt, None), P(wid, None), P(frm, None)),
        out_specs=(P(frm, ("x", "zh", "c")), P(frm, None)),
        check_vma=False,
    )
```

```python
import math

import jax
import jax.numpy as jnp
from jax import lax
from jax.experimental import pallas as pl
from jax.experimental.pallas import tpu as pltpu
from jax.sharding import Mesh, PartitionSpec as P

ITERS = 3
Z_HI = 2
CORES = 2
Z_LO = 4
N_X = 4
LANES = 128
PLANE = ("zh", "y", "zl")
DEEP = ("zh", "zl")
PIVOTS = 4
VMEM = pl.BlockSpec(memory_space=pltpu.VMEM)
SMEM = pl.BlockSpec(memory_space=pltpu.SMEM)
PARAMS = pltpu.CompilerParams(vmem_limit_bytes=40 << 20)
F32 = jnp.float32
HIGHEST = lax.Precision.HIGHEST


def shape(*dims, dtype=F32):
    return jax.ShapeDtypeStruct(dims, dtype)


def gram_kernel(scale, at, blocks, kept, sent, core, acc):
    _, total, depth = blocks.shape
    strip = kept.shape[1]
    for j in range(N_X):
        for x in range(N_X):
            for zh in range(Z_HI):
                for c in range(CORES):
                    source = ((x * Z_HI + zh) * CORES + c) * strip
                    place = ((zh * N_X + x) * CORES + c) * strip
                    core[place : place + strip, j * depth : (j + 1) * depth] = blocks[
                        j, source : source + strip, :
                    ]
    rows = []
    for zh in range(Z_HI):
        start = zh * (total // Z_HI) + at[0] * (CORES * strip)
        rows.append(core[pl.ds(pl.multiple_of(start, 32), CORES * strip), :])
    rows = jnp.concatenate(rows, axis=0)
    mine = at[1]
    wide = 2 * LANES
    for pair in range(total // wide):
        acc[...] = scale * lax.dot_general(
            rows,
            core[pair * wide : (pair + 1) * wide, :],
            (((1,), (1,)), ((), ())),
            preferred_element_type=F32,
        )
        for side in range(2):
            tile = 2 * pair + side
            lanes = slice(side * LANES, (side + 1) * LANES)
            for zh in range(Z_HI):
                base = zh * CORES * strip
                keep_at = pl.multiple_of(base + mine * strip, 8)
                send_at = pl.multiple_of(base + (1 - mine) * strip, 8)
                kept[tile * Z_HI + zh] = acc[pl.ds(keep_at, strip), lanes]
                sent[tile * Z_HI + zh] = acc[pl.ds(send_at, strip), lanes]


def cut_kernel(a, b, out_a, out_b):
    start = 0
    for out in (out_a, out_b):
        pieces, rows, _ = out.shape
        for j in range(pieces):
            out[j] = a[start : start + rows, :] + b[start : start + rows, :]
            start += rows


def sum_kernel(in_a, in_b, out_a, out_b):
    for parts, out in ((in_a, out_a), (in_b, out_b)):
        total = parts[0]
        for j in range(1, parts.shape[0]):
            total = total + parts[j]
        for j in range(out.shape[0]):
            out[j] = total


def put_product(gram, basis, out):
    half = basis.shape[0]
    rank = basis.shape[1] // Z_HI
    low = jnp.dot(gram[:, :half], basis, precision=HIGHEST, preferred_element_type=F32)
    high = jnp.dot(gram[:, half:], basis, precision=HIGHEST, preferred_element_type=F32)
    product = low[:, :rank] + high[:, rank:]
    strip = product.shape[0] // Z_HI
    packed = jnp.concatenate([product[:strip], product[strip:]], axis=1)
    for j in range(out.shape[0]):
        out[j] = packed


def first_kernel(in_a, in_b, basis, gram, out):
    mine, total = gram.shape
    cut = in_a.shape[0]
    for t in range(total // LANES):
        lanes = slice(t * LANES, (t + 1) * LANES)
        low, high = t * mine, (t + 1) * mine
        if low < cut:
            end = min(high, cut)
            gram[: end - low, lanes] = in_a[low:end, :]
        if high > cut:
            begin = max(low, cut)
            gram[begin - low :, lanes] = in_b[begin - cut : high - cut, :]
    put_product(gram[...], basis[...], out)


def inverse_factor(small):
    n = small.shape[0]
    group = 8
    row_id = lax.broadcasted_iota(jnp.int32, (n, n), 0)
    col_id = lax.broadcasted_iota(jnp.int32, (n, n), 1)
    whole = jnp.concatenate([small, (row_id == col_id).astype(F32)], axis=1)
    blocks = [whole[g * group : (g + 1) * group] for g in range(n // group)]
    sub = lax.broadcasted_iota(jnp.int32, (group, 1), 0)
    done = []
    for k in range(0, n, PIVOTS):
        g, i = divmod(k, group)
        live = blocks[g:]
        cols = [
            [jnp.broadcast_to(b[:, k + m : k + m + 1], b.shape) for b in live] for m in range(PIVOTS)
        ]
        rows = [blocks[g][i + m : i + m + 1, :] for m in range(PIVOTS)]
        corner = [[cols[m][0][i + r : i + r + 1, :] for m in range(PIVOTS)] for r in range(PIVOTS)]
        for m in range(PIVOTS):
            inverse = 1.0 / corner[m][m]
            cols[m] = [c * inverse for c in cols[m]]
            for r in range(m + 1, PIVOTS):
                factor = corner[r][m] * inverse
                rows[r] = rows[r] - factor * rows[m]
                for q in range(m + 1, PIVOTS):
                    corner[r][q] = corner[r][q] - factor * corner[m][q]
                cols[r] = [c - w * corner[m][r] for c, w in zip(cols[r], cols[m])]
            done.append(rows[m] * lax.rsqrt(corner[m][m]))
        for at, block in enumerate(live):
            new = block
            for m in range(PIVOTS):
                new = new - cols[m][at] * rows[m]
            if at == 0:
                new = jnp.where(sub >= i + PIVOTS, new, block)
            blocks[g + at] = new
    return jnp.concatenate(done, axis=0)[:, n:]


def factor_of(packed):
    both = lax.dot_general(
        packed, packed, (((0,), (0,)), ((), ())), precision=HIGHEST, preferred_element_type=F32
    )
    rank = both.shape[0] // Z_HI
    inverse = inverse_factor(both[:rank, :rank] + both[rank:, rank:])
    zero = jnp.zeros_like(inverse)
    return jnp.concatenate(
        [jnp.concatenate([inverse, zero], axis=1), jnp.concatenate([zero, inverse], axis=1)], axis=0
    )


def apply_factor(rows, inverse):
    return lax.dot_general(
        rows, inverse, (((1,), (1,)), ((), ())), precision=HIGHEST, preferred_element_type=F32
    )


def step_kernel(packed, gram, out):
    product = packed[...]
    basis = apply_factor(product, factor_of(product))
    put_product(gram[...], basis, out)


def last_kernel(at, packed, out):
    frames, rank = out.shape
    inverse = factor_of(packed[...])
    rows = packed[pl.ds(pl.multiple_of(at[3], 8), frames), :]
    rows = apply_factor(rows, inverse) * math.sqrt(Z_HI * packed.shape[0])
    out[...] = jnp.where(at[2] == 0, rows[:, :rank], rows[:, rank:])


def call(kernel, outs, ins, args, scratch=()):
    return pl.pallas_call(
        kernel,
        out_shape=outs,
        in_specs=ins,
        out_specs=jax.tree.map(lambda _: VMEM, outs),
        scratch_shapes=list(scratch),
        compiler_params=PARAMS,
    )(*args)


def spread(x, axes):
    copies = jnp.broadcast_to(x[None], (lax.axis_size(axes),) + x.shape)
    return lax.all_to_all(copies, axes, 0, 0, tiled=True)


def swap(x, axis):
    return lax.ppermute(x, axis, [(0, 1), (1, 0)])


def local(video, height_factor, width_factor, start_basis):
    rank_h = height_factor.shape[1]
    rank_w = width_factor.shape[1]
    rank_f = start_basis.shape[1]
    frames_dev, _, cols = video.shape
    frm = lax.axis_index(("y", "zl"))
    frm_count = lax.axis_size(("y", "zl"))
    total = frames_dev * frm_count
    x_at, zh_at, core_at = lax.axis_index("x"), lax.axis_index("zh"), lax.axis_index("c")
    first = core_at == 0
    strip = total // (N_X * Z_HI * CORES)
    frame = frm * frames_dev
    frame_zh = frame // (CORES * strip) % Z_HI
    frame_row = (frame // (Z_HI * CORES * strip) * CORES + frame // strip % CORES) * strip + frame % strip
    at = jnp.stack([x_at, core_at, frame_zh, frame_row]).astype(jnp.int32)

    mid = jnp.einsum(
        "fhw,hr->rfw", video, height_factor, preferred_element_type=F32
    ).astype(jnp.bfloat16)
    mid, width, start = lax.optimization_barrier((mid, width_factor, start_basis))
    mid = lax.psum_scatter(mid, "x", scatter_dimension=0, tiled=True)
    width_other = swap(width, "zh")
    basis = spread(start, ("y", "zl")).reshape(N_X, Z_HI, CORES, strip, rank_f)
    basis = basis.transpose(0, 2, 3, 1, 4).reshape(total // Z_HI, Z_HI * rank_f)
    mid, width_other, basis = lax.optimization_barrier((mid, width_other, basis))

    mid = lax.all_to_all(mid, PLANE, 0, 0, tiled=True).reshape(Z_HI, total, cols)
    low_width = jnp.where(zh_at == 0, width, width_other)
    high_width = jnp.where(zh_at == 0, width_other, width)
    part = jnp.dot(mid[0], low_width, preferred_element_type=F32) + jnp.dot(
        mid[1], high_width, preferred_element_type=F32
    )
    half = rank_w // CORES
    low, high = part[:, :half], part[:, half:]
    came = swap(jnp.where(first, high, low).astype(jnp.bfloat16), "c")
    own = jnp.where(first, low, high).astype(jnp.bfloat16)
    core = (own.astype(F32) + came.astype(F32)).astype(jnp.bfloat16)

    blocks = spread(core, "x")
    mine = Z_HI * strip
    tiles = total // LANES
    kept, sent = call(
        lambda *refs: gram_kernel(1.0 / (rank_h * rank_w), *refs),
        [shape(tiles * Z_HI, strip, LANES)] * 2,
        [SMEM, VMEM],
        (at, blocks),
        [
            pltpu.VMEM((total, N_X * half), jnp.bfloat16),
            pltpu.VMEM((total // N_X, 2 * LANES), F32),
        ],
    )
    came = swap(sent, "c")

    flat = tiles * mine
    ring = lax.axis_size("y")
    rows_a = -(-flat // (2 * 8 * ring)) * 8
    rows_b = flat // ring - rows_a
    part_a, part_b = shape(ring, rows_a, LANES), shape(ring, rows_b, LANES)
    sides = call(
        cut_kernel,
        [part_a, part_b],
        [VMEM] * 2,
        (kept.reshape(flat, LANES), came.reshape(flat, LANES)),
    )
    axes = (DEEP, "y")
    sides = [lax.all_to_all(x, axes[i], 0, 0, tiled=True) for i, x in enumerate(sides)]
    sides = call(sum_kernel, [part_a, part_b], [VMEM] * 2, sides)
    sides = [lax.all_to_all(x, axes[1 - i], 0, 0, tiled=True) for i, x in enumerate(sides)]
    sides = call(sum_kernel, [part_a, part_b], [VMEM] * 2, sides)
    sides = [lax.all_to_all(x, axes[i], 0, 0, tiled=True) for i, x in enumerate(sides)]

    packed_shape = shape(N_X * CORES, strip, Z_HI * rank_f)
    gram, packed = call(
        first_kernel,
        [shape(mine, total), packed_shape],
        [VMEM] * 3,
        [x.reshape(-1, LANES) for x in sides] + [basis],
    )
    for step in range(ITERS):
        packed = lax.all_to_all(packed, ("x", "c"), 0, 0, tiled=True)
        packed = packed.reshape(total // Z_HI, Z_HI * rank_f)
        if step < ITERS - 1:
            packed = call(step_kernel, packed_shape, [VMEM] * 2, (packed, gram))
    factor = call(last_kernel, shape(frames_dev, rank_f), [SMEM, VMEM], (at, packed))
    strip_rows = lax.dynamic_slice_in_dim(gram, zh_at * strip, strip, 0)
    column = frame_zh * (total // Z_HI) + frame_row
    gram_out = lax.dynamic_slice_in_dim(strip_rows.T, column, frames_dev, 0)
    return (gram_out, factor)


def solution(mesh):
    frm, hgt, _ = mesh.devices.shape
    fine = Mesh(
        mesh.devices.reshape(frm // Z_LO, Z_LO, hgt, Z_HI, CORES), ("y", "zl", "x", "zh", "c")
    )
    frm, hgt, wid = ("y", "zl"), "x", ("zh", "c")
    return jax.shard_map(
        local,
        mesh=fine,
        in_specs=(P(frm, hgt, wid), P(hgt, None), P(wid, None), P(frm, None)),
        out_specs=(P(frm, ("x", "zh", "c")), P(frm, None)),
        check_vma=False,
    )
```

```python
import math

import jax
import jax.numpy as jnp
from jax import lax
from jax.experimental import pallas as pl
from jax.experimental.pallas import tpu as pltpu
from jax.sharding import Mesh, PartitionSpec as P

ITERS = 3
Z_HI = 2
CORES = 2
Z_LO = 4
N_X = 4
LANES = 128
PLANE = ("zh", "y", "zl")
PIVOTS = 4
VMEM = pl.BlockSpec(memory_space=pltpu.VMEM)
SMEM = pl.BlockSpec(memory_space=pltpu.SMEM)
PARAMS = pltpu.CompilerParams(vmem_limit_bytes=40 << 20)
F32 = jnp.float32
HIGHEST = lax.Precision.HIGHEST


def shape(*dims, dtype=F32):
    return jax.ShapeDtypeStruct(dims, dtype)


def gram_kernel(scale, at, blocks, kept, sent, core, acc):
    _, total, depth = blocks.shape
    strip = kept.shape[1]
    for j in range(N_X):
        for x in range(N_X):
            for zh in range(Z_HI):
                for c in range(CORES):
                    source = ((x * Z_HI + zh) * CORES + c) * strip
                    place = ((zh * N_X + x) * CORES + c) * strip
                    core[place : place + strip, j * depth : (j + 1) * depth] = blocks[
                        j, source : source + strip, :
                    ]
    rows = []
    for zh in range(Z_HI):
        start = zh * (total // Z_HI) + at[0] * (CORES * strip)
        rows.append(core[pl.ds(pl.multiple_of(start, 32), CORES * strip), :])
    rows = jnp.concatenate(rows, axis=0)
    mine = at[1]
    wide = 2 * LANES
    for pair in range(total // wide):
        acc[...] = scale * lax.dot_general(
            rows,
            core[pair * wide : (pair + 1) * wide, :],
            (((1,), (1,)), ((), ())),
            preferred_element_type=F32,
        )
        for side in range(2):
            tile = 2 * pair + side
            lanes = slice(side * LANES, (side + 1) * LANES)
            for zh in range(Z_HI):
                base = zh * CORES * strip
                keep_at = pl.multiple_of(base + mine * strip, 8)
                send_at = pl.multiple_of(base + (1 - mine) * strip, 8)
                kept[tile * Z_HI + zh] = acc[pl.ds(keep_at, strip), lanes]
                sent[tile * Z_HI + zh] = acc[pl.ds(send_at, strip), lanes]


def pack_kernel(a, b, out):
    pieces, rows, _ = out.shape
    for j in range(pieces):
        out[j] = a[j * rows : (j + 1) * rows, :] + b[j * rows : (j + 1) * rows, :]


def sum_kernel(parts, start, out):
    count, rows, _ = parts.shape
    total = parts[0]
    for j in range(1, count):
        total = total + parts[j]
    share = start.shape[0]
    for j in range(count):
        out[j, 0:rows, :] = total
        out[j, rows : rows + share, :] = start[...]


def put_product(gram, basis, out):
    half = basis.shape[0]
    rank = basis.shape[1] // Z_HI
    low = jnp.dot(gram[:, :half], basis, precision=HIGHEST, preferred_element_type=F32)
    high = jnp.dot(gram[:, half:], basis, precision=HIGHEST, preferred_element_type=F32)
    product = low[:, :rank] + high[:, rank:]
    strip = product.shape[0] // Z_HI
    packed = jnp.concatenate([product[:strip], product[strip:]], axis=1)
    for j in range(out.shape[0]):
        out[j] = packed


def first_kernel(rows, pieces, gram, out, flat, basis):
    count, _, _ = pieces.shape
    for j in range(count):
        flat[j * rows : (j + 1) * rows, :] = pieces[j, 0:rows, :]
    mine, total = gram.shape
    for t in range(total // LANES):
        gram[:, t * LANES : (t + 1) * LANES] = flat[t * mine : (t + 1) * mine, :]
    rank = basis.shape[1] // Z_HI
    strip = 4 * basis.shape[0] // (count // Z_HI)
    share = strip // (2 * 2 * Z_HI)
    for j in range(count):
        zh, frm = divmod(j, count // Z_HI)
        place, odd = divmod(frm, 2)
        x, side, c = place // (Z_HI * CORES), place // CORES % Z_HI, place % CORES
        start = (x * CORES + c) * strip + (2 * odd + zh) * (strip // 4)
        block = pieces[j, rows : rows + share, :]
        for part in range(2):
            basis[start + part * share : start + (part + 1) * share, side * rank : (side + 1) * rank] = (
                block[:, part * rank : (part + 1) * rank]
            )
    put_product(gram[...], basis[...], out)


def inverse_factor(small):
    n = small.shape[0]
    group = 8
    row_id = lax.broadcasted_iota(jnp.int32, (n, n), 0)
    col_id = lax.broadcasted_iota(jnp.int32, (n, n), 1)
    whole = jnp.concatenate([small, (row_id == col_id).astype(F32)], axis=1)
    blocks = [whole[g * group : (g + 1) * group] for g in range(n // group)]
    sub = lax.broadcasted_iota(jnp.int32, (group, 1), 0)
    done = []
    for k in range(0, n, PIVOTS):
        g, i = divmod(k, group)
        live = blocks[g:]
        cols = [
            [jnp.broadcast_to(b[:, k + m : k + m + 1], b.shape) for b in live] for m in range(PIVOTS)
        ]
        rows = [blocks[g][i + m : i + m + 1, :] for m in range(PIVOTS)]
        corner = [[cols[m][0][i + r : i + r + 1, :] for m in range(PIVOTS)] for r in range(PIVOTS)]
        for m in range(PIVOTS):
            inverse = 1.0 / corner[m][m]
            cols[m] = [c * inverse for c in cols[m]]
            for r in range(m + 1, PIVOTS):
                factor = corner[r][m] * inverse
                rows[r] = rows[r] - factor * rows[m]
                for q in range(m + 1, PIVOTS):
                    corner[r][q] = corner[r][q] - factor * corner[m][q]
                cols[r] = [c - w * corner[m][r] for c, w in zip(cols[r], cols[m])]
            done.append(rows[m] * lax.rsqrt(corner[m][m]))
        for at, block in enumerate(live):
            new = block
            for m in range(PIVOTS):
                new = new - cols[m][at] * rows[m]
            if at == 0:
                new = jnp.where(sub >= i + PIVOTS, new, block)
            blocks[g + at] = new
    return jnp.concatenate(done, axis=0)[:, n:]


def factor_of(packed):
    both = lax.dot_general(
        packed, packed, (((0,), (0,)), ((), ())), precision=HIGHEST, preferred_element_type=F32
    )
    rank = both.shape[0] // Z_HI
    inverse = inverse_factor(both[:rank, :rank] + both[rank:, rank:])
    zero = jnp.zeros_like(inverse)
    return jnp.concatenate(
        [jnp.concatenate([inverse, zero], axis=1), jnp.concatenate([zero, inverse], axis=1)], axis=0
    )


def apply_factor(rows, inverse):
    return lax.dot_general(
        rows, inverse, (((1,), (1,)), ((), ())), precision=HIGHEST, preferred_element_type=F32
    )


def step_kernel(packed, gram, out):
    product = packed[...]
    basis = apply_factor(product, factor_of(product))
    put_product(gram[...], basis, out)


def last_kernel(at, packed, out):
    frames, rank = out.shape
    inverse = factor_of(packed[...])
    rows = packed[pl.ds(pl.multiple_of(at[3], 8), frames), :]
    rows = apply_factor(rows, inverse) * math.sqrt(Z_HI * packed.shape[0])
    out[...] = jnp.where(at[2] == 0, rows[:, :rank], rows[:, rank:])


def call(kernel, outs, ins, args, scratch=()):
    return pl.pallas_call(
        kernel,
        out_shape=outs,
        in_specs=ins,
        out_specs=jax.tree.map(lambda _: VMEM, outs),
        scratch_shapes=list(scratch),
        compiler_params=PARAMS,
    )(*args)


def spread(x, axes):
    copies = jnp.broadcast_to(x[None], (lax.axis_size(axes),) + x.shape)
    return lax.all_to_all(copies, axes, 0, 0, tiled=True)


def shift(x, by):
    return lax.ppermute(x, "x", [(i, (i + by) % N_X) for i in range(N_X)])


def ring_sum(mid, x_at):
    frames, rank, cols = mid.shape
    block, half = rank // N_X, frames // 2
    ends = []
    for way, first in ((1, 0), (-1, half)):
        total = None
        for step in range(1, N_X + 1):
            at = lax.rem(x_at - way * step + 2 * N_X, N_X) * block
            own = lax.dynamic_slice(mid, (first, at, 0), (half, block, cols))
            if total is not None:
                total = shift(total, way)
                own = (total.astype(F32) + own.astype(F32)).astype(mid.dtype)
            total = own
        ends.append(total)
    return jnp.concatenate(ends, axis=0)


def swap(x, axis):
    return lax.ppermute(x, axis, [(0, 1), (1, 0)])


def local(video, height_factor, width_factor, start_basis):
    rank_h = height_factor.shape[1]
    rank_w = width_factor.shape[1]
    rank_f = start_basis.shape[1]
    frames_dev, _, cols = video.shape
    frm = lax.axis_index(("y", "zl"))
    total = frames_dev * lax.axis_size(("y", "zl"))
    x_at, zh_at, core_at = lax.axis_index("x"), lax.axis_index("zh"), lax.axis_index("c")
    first = core_at == 0
    strip = total // (N_X * Z_HI * CORES)
    frame = frm * frames_dev
    frame_zh = frame // (CORES * strip) % Z_HI
    frame_row = (frame // (Z_HI * CORES * strip) * CORES + frame // strip % CORES) * strip + frame % strip
    at = jnp.stack([x_at, core_at, frame_zh, frame_row]).astype(jnp.int32)

    mid = jnp.einsum(
        "fhw,hr->frw", video, height_factor, preferred_element_type=F32
    ).astype(jnp.bfloat16)
    mid, width = lax.optimization_barrier((mid, width_factor))
    width_other = swap(width, "zh")
    mid = ring_sum(mid, x_at)
    mid, width_other = lax.optimization_barrier((mid, width_other))

    mid = mid.transpose(1, 0, 2)
    mid = lax.all_to_all(mid, PLANE, 0, 0, tiled=True).reshape(Z_HI, total, cols)
    low_width = jnp.where(zh_at == 0, width, width_other)
    high_width = jnp.where(zh_at == 0, width_other, width)
    part = jnp.dot(mid[0], low_width, preferred_element_type=F32) + jnp.dot(
        mid[1], high_width, preferred_element_type=F32
    )
    half = rank_w // CORES
    low, high = part[:, :half], part[:, half:]
    came = swap(jnp.where(first, high, low).astype(jnp.bfloat16), "c")
    own = jnp.where(first, low, high).astype(jnp.bfloat16)
    core = (own.astype(F32) + came.astype(F32)).astype(jnp.bfloat16)

    blocks = spread(core, "x")
    mine = Z_HI * strip
    tiles = total // LANES
    kept, sent = call(
        lambda *refs: gram_kernel(1.0 / (rank_h * rank_w), *refs),
        [shape(tiles * Z_HI, strip, LANES)] * 2,
        [SMEM, VMEM],
        (at, blocks),
        [
            pltpu.VMEM((total, N_X * half), jnp.bfloat16),
            pltpu.VMEM((total // N_X, 2 * LANES), F32),
        ],
    )
    came = swap(sent, "c")

    flat = tiles * mine
    count = lax.axis_size(PLANE)
    rows = flat // count
    pieces = call(
        pack_kernel,
        shape(count, rows, LANES),
        [VMEM] * 2,
        (kept.reshape(flat, LANES), came.reshape(flat, LANES)),
    )
    pieces = lax.all_to_all(pieces, PLANE, 0, 0, tiled=True)
    share = frames_dev // (2 * Z_HI)
    start = lax.dynamic_slice_in_dim(start_basis, zh_at * 2 * share, 2 * share, 0)
    start = jnp.concatenate([start[:share], start[share:]], axis=1)
    padded = -(-(rows + share) // 8) * 8
    pieces = call(sum_kernel, shape(count, padded, LANES), [VMEM] * 2, (pieces, start))
    pieces = lax.all_to_all(pieces, PLANE, 0, 0, tiled=True)

    packed_shape = shape(N_X * CORES, strip, Z_HI * rank_f)
    gram, packed = call(
        lambda *refs: first_kernel(rows, *refs),
        [shape(mine, total), packed_shape],
        [VMEM],
        (pieces,),
        [pltpu.VMEM((flat, LANES), F32), pltpu.VMEM((total // Z_HI, Z_HI * rank_f), F32)],
    )
    for step in range(ITERS):
        packed = lax.all_to_all(packed, ("x", "c"), 0, 0, tiled=True)
        packed = packed.reshape(total // Z_HI, Z_HI * rank_f)
        if step < ITERS - 1:
            packed = call(step_kernel, packed_shape, [VMEM] * 2, (packed, gram))
    factor = call(last_kernel, shape(frames_dev, rank_f), [SMEM, VMEM], (at, packed))
    strip_rows = lax.dynamic_slice_in_dim(gram, zh_at * strip, strip, 0)
    column = frame_zh * (total // Z_HI) + frame_row
    gram_out = lax.dynamic_slice_in_dim(strip_rows.T, column, frames_dev, 0)
    return (gram_out, factor)


def solution(mesh):
    frm, hgt, _ = mesh.devices.shape
    fine = Mesh(
        mesh.devices.reshape(frm // Z_LO, Z_LO, hgt, Z_HI, CORES), ("y", "zl", "x", "zh", "c")
    )
    frm, hgt, wid = ("y", "zl"), "x", ("zh", "c")
    return jax.shard_map(
        local,
        mesh=fine,
        in_specs=(P(frm, hgt, wid), P(hgt, None), P(wid, None), P(frm, None)),
        out_specs=(P(frm, ("x", "zh", "c")), P(frm, None)),
        check_vma=False,
    )
```

```python
import math

import jax
import jax.numpy as jnp
from jax import lax
from jax.experimental import pallas as pl
from jax.experimental.pallas import tpu as pltpu
from jax.sharding import Mesh, PartitionSpec as P

ITERS = 3
Z_HI = 2
CORES = 2
Z_LO = 4
N_X = 4
LANES = 128
FRM = ("y", "zl")
PLANE = ("zh", "y", "zl")
PIVOTS = 4
VMEM = pl.BlockSpec(memory_space=pltpu.VMEM)
SMEM = pl.BlockSpec(memory_space=pltpu.SMEM)
PARAMS = pltpu.CompilerParams(vmem_limit_bytes=40 << 20)
F32 = jnp.float32
HIGHEST = lax.Precision.HIGHEST


def shape(*dims, dtype=F32):
    return jax.ShapeDtypeStruct(dims, dtype)


def pick_kernel(at, mid, out_a, out_b):
    for way, first, out in ((1, 0, out_a), (-1, mid.shape[0] // 2, out_b)):
        ring_block(at, mid, 1, way, first, out, None)


def ring_block(at, mid, step, way, first, out, came):
    half, block, _ = out.shape
    start = pl.multiple_of(lax.rem(at[0] - way * step + 2 * N_X, N_X) * block, 64)
    for f in range(half):
        own = mid[first + f, pl.ds(start, block), :]
        if came is not None:
            own = (own.astype(F32) + came[f].astype(F32)).astype(out.dtype)
        out[f] = own


def core_kernel(at, mid, width, width_other, own, sent):
    half = own.shape[1]
    zh = at[4]
    part = jnp.dot(mid[zh], width[...], preferred_element_type=F32) + jnp.dot(
        mid[1 - zh], width_other[...], preferred_element_type=F32
    )
    low, high = part[:, :half].astype(own.dtype), part[:, half:].astype(own.dtype)
    first = at[1] == 0

    @pl.when(first)
    def _():
        own[...] = low
        sent[...] = high

    @pl.when(jnp.logical_not(first))
    def _():
        own[...] = high
        sent[...] = low


def copies_kernel(a, b, out):
    total = (a[...].astype(F32) + b[...].astype(F32)).astype(out.dtype)
    for j in range(out.shape[0]):
        out[j] = total


def gram_kernel(scale, at, blocks, kept, sent, core, acc):
    _, total, depth = blocks.shape
    strip = kept.shape[1]
    for j in range(N_X):
        for x in range(N_X):
            for zh in range(Z_HI):
                for c in range(CORES):
                    source = ((x * Z_HI + zh) * CORES + c) * strip
                    place = ((zh * N_X + x) * CORES + c) * strip
                    core[place : place + strip, j * depth : (j + 1) * depth] = blocks[
                        j, source : source + strip, :
                    ]
    rows = []
    for zh in range(Z_HI):
        start = zh * (total // Z_HI) + at[0] * (CORES * strip)
        rows.append(core[pl.ds(pl.multiple_of(start, 32), CORES * strip), :])
    rows = jnp.concatenate(rows, axis=0)
    mine = at[1]
    wide = 2 * LANES
    for pair in range(total // wide):
        acc[...] = scale * lax.dot_general(
            rows,
            core[pair * wide : (pair + 1) * wide, :],
            (((1,), (1,)), ((), ())),
            preferred_element_type=F32,
        )
        for side in range(2):
            tile = 2 * pair + side
            lanes = slice(side * LANES, (side + 1) * LANES)
            for zh in range(Z_HI):
                base = zh * CORES * strip
                keep_at = pl.multiple_of(base + mine * strip, 8)
                send_at = pl.multiple_of(base + (1 - mine) * strip, 8)
                kept[tile * Z_HI + zh] = acc[pl.ds(keep_at, strip), lanes]
                sent[tile * Z_HI + zh] = acc[pl.ds(send_at, strip), lanes]


def sum_kernel(rows, parts, out):
    count = parts.shape[0] // rows
    total = parts[0:rows, :]
    for j in range(1, count):
        total = total + parts[j * rows : (j + 1) * rows, :]
    for j in range(count):
        out[j * rows : (j + 1) * rows, :] = total


def put_product(gram, basis, out):
    half = basis.shape[0]
    rank = basis.shape[1] // Z_HI
    low = jnp.dot(gram[:, :half], basis, precision=HIGHEST, preferred_element_type=F32)
    high = jnp.dot(gram[:, half:], basis, precision=HIGHEST, preferred_element_type=F32)
    product = low[:, :rank] + high[:, rank:]
    strip = product.shape[0] // Z_HI
    packed = jnp.concatenate([product[:strip], product[strip:]], axis=1)
    for j in range(out.shape[0]):
        out[j] = packed


def first_kernel(flat, shards, gram, out, basis):
    mine, total = gram.shape
    for t in range(total // LANES):
        gram[:, t * LANES : (t + 1) * LANES] = flat[t * mine : (t + 1) * mine, :]
    rank = basis.shape[1] // Z_HI
    strip = total // (N_X * Z_HI * CORES)
    half = strip // 4
    for frm in range(total // (2 * half)):
        place, odd = divmod(frm, 2)
        x, side, c = place // (Z_HI * CORES), place // CORES % Z_HI, place % CORES
        for part in range(2):
            start = (x * CORES + c) * strip + (2 * odd + part) * half
            basis[start : start + half, side * rank : (side + 1) * rank] = shards[
                frm * half : (frm + 1) * half, part * rank : (part + 1) * rank
            ]
    put_product(gram[...], basis[...], out)


def inverse_factor(small):
    n = small.shape[0]
    group = 8
    row_id = lax.broadcasted_iota(jnp.int32, (n, n), 0)
    col_id = lax.broadcasted_iota(jnp.int32, (n, n), 1)
    whole = jnp.concatenate([small, (row_id == col_id).astype(F32)], axis=1)
    blocks = [whole[g * group : (g + 1) * group] for g in range(n // group)]
    sub = lax.broadcasted_iota(jnp.int32, (group, 1), 0)
    done = []
    for k in range(0, n, PIVOTS):
        g, i = divmod(k, group)
        live = blocks[g:]
        cols = [
            [jnp.broadcast_to(b[:, k + m : k + m + 1], b.shape) for b in live] for m in range(PIVOTS)
        ]
        rows = [blocks[g][i + m : i + m + 1, :] for m in range(PIVOTS)]
        corner = [[cols[m][0][i + r : i + r + 1, :] for m in range(PIVOTS)] for r in range(PIVOTS)]
        for m in range(PIVOTS):
            inverse = 1.0 / corner[m][m]
            cols[m] = [c * inverse for c in cols[m]]
            for r in range(m + 1, PIVOTS):
                factor = corner[r][m] * inverse
                rows[r] = rows[r] - factor * rows[m]
                for q in range(m + 1, PIVOTS):
                    corner[r][q] = corner[r][q] - factor * corner[m][q]
                cols[r] = [c - w * corner[m][r] for c, w in zip(cols[r], cols[m])]
            done.append(rows[m] * lax.rsqrt(corner[m][m]))
        for at, block in enumerate(live):
            new = block
            for m in range(PIVOTS):
                new = new - cols[m][at] * rows[m]
            if at == 0:
                new = jnp.where(sub >= i + PIVOTS, new, block)
            blocks[g + at] = new
    return jnp.concatenate(done, axis=0)[:, n:]


def factor_of(packed):
    both = lax.dot_general(
        packed, packed, (((0,), (0,)), ((), ())), precision=HIGHEST, preferred_element_type=F32
    )
    rank = both.shape[0] // Z_HI
    inverse = inverse_factor(both[:rank, :rank] + both[rank:, rank:])
    zero = jnp.zeros_like(inverse)
    return jnp.concatenate(
        [jnp.concatenate([inverse, zero], axis=1), jnp.concatenate([zero, inverse], axis=1)], axis=0
    )


def apply_factor(rows, inverse):
    return lax.dot_general(
        rows, inverse, (((1,), (1,)), ((), ())), precision=HIGHEST, preferred_element_type=F32
    )


def step_kernel(packed, gram, out):
    product = packed[...]
    basis = apply_factor(product, factor_of(product))
    put_product(gram[...], basis, out)


def last_kernel(at, packed, out):
    frames, rank = out.shape
    inverse = factor_of(packed[...])
    rows = packed[pl.ds(pl.multiple_of(at[3], 8), frames), :]
    rows = apply_factor(rows, inverse) * math.sqrt(Z_HI * packed.shape[0])
    out[...] = jnp.where(at[2] == 0, rows[:, :rank], rows[:, rank:])


def call(kernel, outs, ins, args, scratch=()):
    return pl.pallas_call(
        kernel,
        out_shape=outs,
        in_specs=ins,
        out_specs=jax.tree.map(lambda _: VMEM, outs),
        scratch_shapes=list(scratch),
        compiler_params=PARAMS,
    )(*args)


def trade(x, axes):
    count = lax.axis_size(axes)
    rows = lax.all_to_all(x.reshape(count, 1, -1), axes, 0, 0, tiled=True)
    return rows.reshape(x.shape)


def shift(x, by):
    return lax.ppermute(x, "x", [(i, (i + by) % N_X) for i in range(N_X)])


def swap(x, axis):
    return lax.ppermute(x, axis, [(0, 1), (1, 0)])


def ring_sum(mid, at):
    frames, rank, cols = mid.shape
    piece = shape(frames // 2, rank // N_X, cols, dtype=mid.dtype)
    ends = list(call(pick_kernel, [piece, piece], [SMEM, VMEM], (at, mid)))
    ways = ((1, 0), (-1, frames // 2))
    for step in range(2, N_X + 1):
        for i, (way, first) in enumerate(ways):

            def kernel(at, came, mid, out, way=way, first=first, step=step):
                ring_block(at, mid, step, way, first, out, came)

            ends[i] = call(kernel, piece, [SMEM, VMEM, VMEM], (at, shift(ends[i], way), mid))
    return jnp.concatenate(ends, axis=0)


def local(video, height_factor, width_factor, start_basis):
    rank_h = height_factor.shape[1]
    rank_w = width_factor.shape[1]
    rank_f = start_basis.shape[1]
    frames_dev, _, cols = video.shape
    frm = lax.axis_index(FRM)
    total = frames_dev * lax.axis_size(FRM)
    x_at, zh_at, core_at = lax.axis_index("x"), lax.axis_index("zh"), lax.axis_index("c")
    strip = total // (N_X * Z_HI * CORES)
    frame = frm * frames_dev
    frame_zh = frame // (CORES * strip) % Z_HI
    frame_row = (frame // (Z_HI * CORES * strip) * CORES + frame // strip % CORES) * strip + frame % strip
    at = jnp.stack([x_at, core_at, frame_zh, frame_row, zh_at]).astype(jnp.int32)

    mid = jnp.einsum(
        "fhw,hr->frw", video, height_factor, preferred_element_type=F32
    ).astype(jnp.bfloat16)
    mid = ring_sum(mid, at).transpose(1, 0, 2)

    mid, width = lax.optimization_barrier((mid, width_factor))
    width_other = swap(width, "zh")
    mid = lax.all_to_all(mid, PLANE, 0, 0, tiled=True).reshape(Z_HI, total, cols)
    half = rank_w // CORES
    own, sent = call(
        core_kernel,
        [shape(total, half, dtype=mid.dtype)] * 2,
        [SMEM] + [VMEM] * 3,
        (at, mid, width, width_other),
    )

    copies = call(
        copies_kernel, shape(N_X, total, half, dtype=mid.dtype), [VMEM] * 2, (own, swap(sent, "c"))
    )
    part = frames_dev // 2
    start = jnp.concatenate([start_basis[:part], start_basis[part:]], axis=1).reshape(1, -1)
    start = jnp.broadcast_to(start[None], (lax.axis_size(FRM),) + start.shape)
    copies, start = lax.optimization_barrier((copies, start))
    blocks = lax.all_to_all(copies, "x", 0, 0, tiled=True)
    shards = lax.all_to_all(start, FRM, 0, 0, tiled=True).reshape(-1, LANES)
    blocks, shards = lax.optimization_barrier((blocks, shards))
    mine = Z_HI * strip
    tiles = total // LANES
    kept, sent = call(
        lambda *refs: gram_kernel(1.0 / (rank_h * rank_w), *refs),
        [shape(tiles * Z_HI, strip, LANES)] * 2,
        [SMEM, VMEM],
        (at, blocks),
        [
            pltpu.VMEM((total, N_X * half), jnp.bfloat16),
            pltpu.VMEM((total // N_X, 2 * LANES), F32),
        ],
    )
    came = swap(sent, "c")

    flat = shape(tiles * mine, LANES)
    pieces = trade(kept.reshape(flat.shape) + came.reshape(flat.shape), PLANE)
    rows = flat.shape[0] // lax.axis_size(PLANE)
    pieces = call(lambda *refs: sum_kernel(rows, *refs), flat, [VMEM], (pieces,))
    pieces = trade(pieces, PLANE)

    packed_shape = shape(N_X * CORES, strip, Z_HI * rank_f)
    gram, packed = call(
        first_kernel,
        [shape(mine, total), packed_shape],
        [VMEM] * 2,
        (pieces, shards),
        [pltpu.VMEM((total // Z_HI, Z_HI * rank_f), F32)],
    )
    for step in range(ITERS):
        packed = lax.all_to_all(packed, ("x", "c"), 0, 0, tiled=True)
        packed = packed.reshape(total // Z_HI, Z_HI * rank_f)
        if step < ITERS - 1:
            packed = call(step_kernel, packed_shape, [VMEM] * 2, (packed, gram))
    factor = call(last_kernel, shape(frames_dev, rank_f), [SMEM, VMEM], (at, packed))
    strip_rows = lax.dynamic_slice_in_dim(gram, zh_at * strip, strip, 0)
    column = frame_zh * (total // Z_HI) + frame_row
    gram_out = lax.dynamic_slice_in_dim(strip_rows.T, column, frames_dev, 0)
    return (gram_out, factor)


def solution(mesh):
    frm, hgt, _ = mesh.devices.shape
    fine = Mesh(
        mesh.devices.reshape(frm // Z_LO, Z_LO, hgt, Z_HI, CORES), ("y", "zl", "x", "zh", "c")
    )
    frm, hgt, wid = ("y", "zl"), "x", ("zh", "c")
    return jax.shard_map(
        local,
        mesh=fine,
        in_specs=(P(frm, hgt, wid), P(hgt, None), P(wid, None), P(frm, None)),
        out_specs=(P(frm, ("x", "zh", "c")), P(frm, None)),
        check_vma=False,
    )
```

```python
import math

import jax
import jax.numpy as jnp
from jax import lax
from jax.experimental import pallas as pl
from jax.experimental.pallas import tpu as pltpu
from jax.sharding import Mesh, PartitionSpec as P

ITERS = 3
Z_HI = 2
CORES = 2
Z_LO = 4
N_X = 4
LANES = 128
FRM = ("y", "zl")
PLANE = ("zh", "y", "zl")
PIVOTS = 4
VMEM = pl.BlockSpec(memory_space=pltpu.VMEM)
SMEM = pl.BlockSpec(memory_space=pltpu.SMEM)
PARAMS = pltpu.CompilerParams(vmem_limit_bytes=40 << 20)
F32 = jnp.float32
HIGHEST = lax.Precision.HIGHEST


def shape(*dims, dtype=F32):
    return jax.ShapeDtypeStruct(dims, dtype)


def pick_kernel(at, mid, out_a, out_b):
    for way, first, out in ((1, 0, out_a), (-1, mid.shape[0] // 2, out_b)):
        ring_block(at, mid, 1, way, first, out, None)


def ring_block(at, mid, step, way, first, out, came):
    half, block, _ = out.shape
    start = pl.multiple_of(lax.rem(at[0] - way * step + 2 * N_X, N_X) * block, 64)
    for f in range(half):
        own = mid[first + f, pl.ds(start, block), :]
        if came is not None:
            own = (own.astype(F32) + came[f].astype(F32)).astype(out.dtype)
        out[f] = own


def add_kernel(a, b, out):
    out[...] = (a[...].astype(F32) + b[...].astype(F32)).astype(out.dtype)


def core_kernel(at, mid, width, width_other, own, sent):
    half = own.shape[1]
    zh = at[4]
    part = jnp.dot(mid[zh], width[...], preferred_element_type=F32) + jnp.dot(
        mid[1 - zh], width_other[...], preferred_element_type=F32
    )
    low, high = part[:, :half].astype(own.dtype), part[:, half:].astype(own.dtype)
    first = at[1] == 0

    @pl.when(first)
    def _():
        own[...] = low
        sent[...] = high

    @pl.when(jnp.logical_not(first))
    def _():
        own[...] = high
        sent[...] = low


def gram_kernel(scale, at, own, left, right, far_a, far_b, kept, sent, core, acc):
    total, depth = own.shape
    far = total // 2
    strip = kept.shape[1]
    for j in range(N_X):
        for x in range(N_X):
            for zh in range(Z_HI):
                for c in range(CORES):
                    source = ((x * Z_HI + zh) * CORES + c) * strip
                    place = ((zh * N_X + x) * CORES + c) * strip
                    if j == N_X - 1:
                        block = far_a if source < far else far_b
                        source = source % far
                    else:
                        block = (own, left, right)[j]
                    core[place : place + strip, j * depth : (j + 1) * depth] = block[
                        source : source + strip, :
                    ]
    rows = []
    for zh in range(Z_HI):
        start = zh * (total // Z_HI) + at[0] * (CORES * strip)
        rows.append(core[pl.ds(pl.multiple_of(start, 32), CORES * strip), :])
    rows = jnp.concatenate(rows, axis=0)
    mine = at[1]
    wide = 2 * LANES
    for pair in range(total // wide):
        acc[...] = scale * lax.dot_general(
            rows,
            core[pair * wide : (pair + 1) * wide, :],
            (((1,), (1,)), ((), ())),
            preferred_element_type=F32,
        )
        for side in range(2):
            tile = 2 * pair + side
            lanes = slice(side * LANES, (side + 1) * LANES)
            for zh in range(Z_HI):
                base = zh * CORES * strip
                keep_at = pl.multiple_of(base + mine * strip, 8)
                send_at = pl.multiple_of(base + (1 - mine) * strip, 8)
                kept[tile * Z_HI + zh] = acc[pl.ds(keep_at, strip), lanes]
                sent[tile * Z_HI + zh] = acc[pl.ds(send_at, strip), lanes]


def put_scaled(x, out, base, rows, step):
    largest = jnp.max(jnp.max(jnp.abs(x), axis=0, keepdims=True), axis=1, keepdims=True)
    exponent = jnp.floor(jnp.log2(jnp.maximum(largest, 2.0**-100))) - 14.0
    scale = jnp.exp2(-exponent)
    tail = jnp.broadcast_to(exponent, (step - rows, x.shape[1]))
    for j in range(x.shape[0] // rows):
        at = base + j * step
        out[at : at + rows, :] = x[j * rows : (j + 1) * rows, :] * scale
        out[at + rows : at + step, :] = tail


def pack_kernel(rows, step, a, b, out):
    put_scaled(a[...] + b[...], out, 0, rows, step)


def unscaled(parts, j, rows, step):
    at = j * step
    return parts[at : at + rows, :] * jnp.exp2(parts[at + rows : at + rows + 1, :])


def sum_kernel(rows, step, parts, out):
    total = unscaled(parts, 0, rows, step)
    for j in range(1, parts.shape[0] // step):
        total = total + unscaled(parts, j, rows, step)
    put_scaled(total, out, 0, rows, step)


def put_product(gram, basis, out):
    half = basis.shape[0]
    rank = basis.shape[1] // Z_HI
    low = jnp.dot(gram[:, :half], basis, precision=HIGHEST, preferred_element_type=F32)
    high = jnp.dot(gram[:, half:], basis, precision=HIGHEST, preferred_element_type=F32)
    product = low[:, :rank] + high[:, rank:]
    strip = product.shape[0] // Z_HI
    packed = jnp.concatenate([product[:strip], product[strip:]], axis=1)
    for j in range(out.shape[0]):
        out[j] = packed


def first_kernel(rows, step, pieces, shards, gram, out, flat, basis):
    for j in range(pieces.shape[0] // step):
        flat[j * rows : (j + 1) * rows, :] = unscaled(pieces, j, rows, step)
    mine, total = gram.shape
    for t in range(total // LANES):
        gram[:, t * LANES : (t + 1) * LANES] = flat[t * mine : (t + 1) * mine, :]
    rank = basis.shape[1] // Z_HI
    strip = total // (N_X * Z_HI * CORES)
    half = strip // 4
    for frm in range(total // (2 * half)):
        place, odd = divmod(frm, 2)
        x, side, c = place // (Z_HI * CORES), place // CORES % Z_HI, place % CORES
        for part in range(2):
            start = (x * CORES + c) * strip + (2 * odd + part) * half
            basis[start : start + half, side * rank : (side + 1) * rank] = shards[
                frm * half : (frm + 1) * half, part * rank : (part + 1) * rank
            ]
    put_product(gram[...], basis[...], out)


def inverse_factor(small):
    n = small.shape[0]
    group = 8
    row_id = lax.broadcasted_iota(jnp.int32, (n, n), 0)
    col_id = lax.broadcasted_iota(jnp.int32, (n, n), 1)
    whole = jnp.concatenate([small, (row_id == col_id).astype(F32)], axis=1)
    blocks = [whole[g * group : (g + 1) * group] for g in range(n // group)]
    sub = lax.broadcasted_iota(jnp.int32, (group, 1), 0)
    done = []
    for k in range(0, n, PIVOTS):
        g, i = divmod(k, group)
        live = blocks[g:]
        cols = [
            [jnp.broadcast_to(b[:, k + m : k + m + 1], b.shape) for b in live] for m in range(PIVOTS)
        ]
        rows = [blocks[g][i + m : i + m + 1, :] for m in range(PIVOTS)]
        corner = [[cols[m][0][i + r : i + r + 1, :] for m in range(PIVOTS)] for r in range(PIVOTS)]
        for m in range(PIVOTS):
            inverse = 1.0 / corner[m][m]
            cols[m] = [c * inverse for c in cols[m]]
            for r in range(m + 1, PIVOTS):
                factor = corner[r][m] * inverse
                rows[r] = rows[r] - factor * rows[m]
                for q in range(m + 1, PIVOTS):
                    corner[r][q] = corner[r][q] - factor * corner[m][q]
                cols[r] = [c - w * corner[m][r] for c, w in zip(cols[r], cols[m])]
            done.append(rows[m] * lax.rsqrt(corner[m][m]))
        for at, block in enumerate(live):
            new = block
            for m in range(PIVOTS):
                new = new - cols[m][at] * rows[m]
            if at == 0:
                new = jnp.where(sub >= i + PIVOTS, new, block)
            blocks[g + at] = new
    return jnp.concatenate(done, axis=0)[:, n:]


def factor_of(packed):
    both = lax.dot_general(
        packed, packed, (((0,), (0,)), ((), ())), precision=HIGHEST, preferred_element_type=F32
    )
    rank = both.shape[0] // Z_HI
    inverse = inverse_factor(both[:rank, :rank] + both[rank:, rank:])
    zero = jnp.zeros_like(inverse)
    return jnp.concatenate(
        [jnp.concatenate([inverse, zero], axis=1), jnp.concatenate([zero, inverse], axis=1)], axis=0
    )


def apply_factor(rows, inverse):
    return lax.dot_general(
        rows, inverse, (((1,), (1,)), ((), ())), precision=HIGHEST, preferred_element_type=F32
    )


def step_kernel(packed, gram, out):
    product = packed[...]
    basis = apply_factor(product, factor_of(product))
    put_product(gram[...], basis, out)


def last_kernel(at, packed, out):
    frames, rank = out.shape
    inverse = factor_of(packed[...])
    rows = packed[pl.ds(pl.multiple_of(at[3], 8), frames), :]
    rows = apply_factor(rows, inverse) * math.sqrt(Z_HI * packed.shape[0])
    out[...] = jnp.where(at[2] == 0, rows[:, :rank], rows[:, rank:])


def call(kernel, outs, ins, args, scratch=()):
    return pl.pallas_call(
        kernel,
        out_shape=outs,
        in_specs=ins,
        out_specs=jax.tree.map(lambda _: VMEM, outs),
        scratch_shapes=list(scratch),
        compiler_params=PARAMS,
    )(*args)


def trade(x, count, axes):
    blocks = lax.all_to_all(x.reshape(count, -1, LANES), axes, 0, 0, tiled=True)
    return blocks.reshape(-1, LANES).astype(F32)


def shift(x, by):
    return lax.ppermute(x, "x", [(i, (i + by) % N_X) for i in range(N_X)])


def swap(x, axis):
    return lax.ppermute(x, axis, [(0, 1), (1, 0)])


def ring_sum(mid, at):
    frames, rank, cols = mid.shape
    piece = shape(frames // 2, rank // N_X, cols, dtype=mid.dtype)
    ends = list(call(pick_kernel, [piece, piece], [SMEM, VMEM], (at, mid)))
    ways = ((1, 0), (-1, frames // 2))
    for step in range(2, N_X + 1):
        for i, (way, first) in enumerate(ways):

            def kernel(at, came, mid, out, way=way, first=first, step=step):
                ring_block(at, mid, step, way, first, out, came)

            ends[i] = call(kernel, piece, [SMEM, VMEM, VMEM], (at, shift(ends[i], way), mid))
    return jnp.concatenate(ends, axis=0)


def local(video, height_factor, width_factor, start_basis):
    rank_h = height_factor.shape[1]
    rank_w = width_factor.shape[1]
    rank_f = start_basis.shape[1]
    frames_dev, _, cols = video.shape
    frm = lax.axis_index(FRM)
    total = frames_dev * lax.axis_size(FRM)
    x_at, zh_at, core_at = lax.axis_index("x"), lax.axis_index("zh"), lax.axis_index("c")
    strip = total // (N_X * Z_HI * CORES)
    frame = frm * frames_dev
    frame_zh = frame // (CORES * strip) % Z_HI
    frame_row = (frame // (Z_HI * CORES * strip) * CORES + frame // strip % CORES) * strip + frame % strip
    at = jnp.stack([x_at, core_at, frame_zh, frame_row, zh_at]).astype(jnp.int32)

    mid = jnp.einsum(
        "fhw,hr->frw", video, height_factor, preferred_element_type=F32
    ).astype(jnp.bfloat16)
    mid = ring_sum(mid, at).transpose(1, 0, 2)

    mid, width = lax.optimization_barrier((mid, width_factor))
    width_other = swap(width, "zh")
    mid = lax.all_to_all(mid, PLANE, 0, 0, tiled=True).reshape(Z_HI, total, cols)
    half = rank_w // CORES
    own, sent = call(
        core_kernel,
        [shape(total, half, dtype=mid.dtype)] * 2,
        [SMEM] + [VMEM] * 3,
        (at, mid, width, width_other),
    )

    core = call(
        add_kernel, shape(total, half, dtype=mid.dtype), [VMEM] * 2, (own, swap(sent, "c"))
    )

    part = frames_dev // 2
    start = jnp.concatenate([start_basis[:part], start_basis[part:]], axis=1).reshape(1, -1)
    start = jnp.broadcast_to(start[None], (lax.axis_size(FRM),) + start.shape)
    core, start = lax.optimization_barrier((core, start))
    left, right = shift(core, 1), shift(core, -1)
    shards = lax.all_to_all(start, FRM, 0, 0, tiled=True).reshape(-1, LANES)
    far_a, far_b = shift(left[: total // 2], 1), shift(right[total // 2 :], -1)
    far_a, far_b, shards = lax.optimization_barrier((far_a, far_b, shards))
    mine = Z_HI * strip
    tiles = total // LANES
    kept, sent = call(
        lambda *refs: gram_kernel(1.0 / (rank_h * rank_w), *refs),
        [shape(tiles * Z_HI, strip, LANES)] * 2,
        [SMEM] + [VMEM] * 5,
        (at, core, left, right, far_a, far_b),
        [
            pltpu.VMEM((total, N_X * half), jnp.bfloat16),
            pltpu.VMEM((total // N_X, 2 * LANES), F32),
        ],
    )
    came = swap(sent, "c")

    flat = shape(tiles * mine, LANES)
    count = lax.axis_size(PLANE)
    rows = flat.shape[0] // count
    step = -(-(rows + 1) // 16) * 16
    pieces = call(
        lambda *refs: pack_kernel(rows, step, *refs),
        shape(count * step, LANES),
        [VMEM] * 2,
        (kept.reshape(flat.shape), came.reshape(flat.shape)),
    )
    pieces = trade(pieces.astype(jnp.float16), count, PLANE)
    piece = call(
        lambda *refs: sum_kernel(rows, step, *refs), shape(step, LANES), [VMEM], (pieces,)
    )
    piece = piece.astype(jnp.float16)
    pieces = trade(jnp.broadcast_to(piece[None], (count,) + piece.shape), count, PLANE)

    packed_shape = shape(N_X * CORES, strip, Z_HI * rank_f)
    gram, packed = call(
        lambda *refs: first_kernel(rows, step, *refs),
        [shape(mine, total), packed_shape],
        [VMEM] * 2,
        (pieces, shards),
        [pltpu.VMEM(flat.shape, F32), pltpu.VMEM((total // Z_HI, Z_HI * rank_f), F32)],
    )
    for step in range(ITERS):
        packed = lax.all_to_all(packed, ("x", "c"), 0, 0, tiled=True)
        packed = packed.reshape(total // Z_HI, Z_HI * rank_f)
        if step < ITERS - 1:
            packed = call(step_kernel, packed_shape, [VMEM] * 2, (packed, gram))
    factor = call(last_kernel, shape(frames_dev, rank_f), [SMEM, VMEM], (at, packed))
    strip_rows = lax.dynamic_slice_in_dim(gram, zh_at * strip, strip, 0)
    column = frame_zh * (total // Z_HI) + frame_row
    gram_out = lax.dynamic_slice_in_dim(strip_rows.T, column, frames_dev, 0)
    return (gram_out, factor)


def solution(mesh):
    frm, hgt, _ = mesh.devices.shape
    fine = Mesh(
        mesh.devices.reshape(frm // Z_LO, Z_LO, hgt, Z_HI, CORES), ("y", "zl", "x", "zh", "c")
    )
    frm, hgt, wid = ("y", "zl"), "x", ("zh", "c")
    return jax.shard_map(
        local,
        mesh=fine,
        in_specs=(P(frm, hgt, wid), P(hgt, None), P(wid, None), P(frm, None)),
        out_specs=(P(frm, ("x", "zh", "c")), P(frm, None)),
        check_vma=False,
    )
```

```python
import math

import jax
import jax.numpy as jnp
from jax import lax
from jax.experimental import pallas as pl
from jax.experimental.pallas import tpu as pltpu
from jax.sharding import Mesh, PartitionSpec as P

ITERS = 3
Z_HI = 2
CORES = 2
Z_LO = 4
N_X = 4
LANES = 128
FRM = ("y", "zl")
PLANE = ("zh", "y", "zl")
PIVOTS = 4
VMEM = pl.BlockSpec(memory_space=pltpu.VMEM)
SMEM = pl.BlockSpec(memory_space=pltpu.SMEM)
PARAMS = pltpu.CompilerParams(vmem_limit_bytes=40 << 20)
F32 = jnp.float32
HIGHEST = lax.Precision.HIGHEST


def shape(*dims, dtype=F32):
    return jax.ShapeDtypeStruct(dims, dtype)


def pick_kernel(at, mid, out_a, out_b):
    for way, first, out in ((1, 0, out_a), (-1, mid.shape[0] // 2, out_b)):
        ring_block(at, mid, 1, way, first, out, None)


def ring_block(at, mid, step, way, first, out, came):
    half, block, _ = out.shape
    start = pl.multiple_of(lax.rem(at[0] - way * step + 2 * N_X, N_X) * block, 64)
    for f in range(half):
        own = mid[first + f, pl.ds(start, block), :]
        if came is not None:
            own = (own.astype(F32) + came[f].astype(F32)).astype(out.dtype)
        out[f] = own


def pass_kernel(at, left, right, out):
    @pl.when(at[1] == 0)
    def _():
        out[...] = left[...]

    @pl.when(at[1] != 0)
    def _():
        out[...] = right[...]


def add_kernel(a, b, out):
    out[...] = (a[...].astype(F32) + b[...].astype(F32)).astype(out.dtype)


def core_kernel(at, mid, width, width_other, own, sent):
    half = own.shape[1]
    zh = at[4]
    part = jnp.dot(mid[zh], width[...], preferred_element_type=F32) + jnp.dot(
        mid[1 - zh], width_other[...], preferred_element_type=F32
    )
    low, high = part[:, :half].astype(own.dtype), part[:, half:].astype(own.dtype)
    first = at[1] == 0

    @pl.when(first)
    def _():
        own[...] = low
        sent[...] = high

    @pl.when(jnp.logical_not(first))
    def _():
        own[...] = high
        sent[...] = low


def gram_kernel(scale, at, own, left, right, far, kept, sent, core, acc):
    total, depth = own.shape
    strip = kept.shape[1]
    for j, block in enumerate((own, left, right, far)):
        for x in range(N_X):
            for zh in range(Z_HI):
                for c in range(CORES):
                    source = ((x * Z_HI + zh) * CORES + c) * strip
                    place = ((zh * N_X + x) * CORES + c) * strip
                    core[place : place + strip, j * depth : (j + 1) * depth] = block[
                        source : source + strip, :
                    ]
    rows = []
    for zh in range(Z_HI):
        start = zh * (total // Z_HI) + at[0] * (CORES * strip)
        rows.append(core[pl.ds(pl.multiple_of(start, 32), CORES * strip), :])
    rows = jnp.concatenate(rows, axis=0)
    mine = at[1]
    wide = 2 * LANES
    for pair in range(total // wide):
        acc[...] = scale * lax.dot_general(
            rows,
            core[pair * wide : (pair + 1) * wide, :],
            (((1,), (1,)), ((), ())),
            preferred_element_type=F32,
        )
        for side in range(2):
            tile = 2 * pair + side
            lanes = slice(side * LANES, (side + 1) * LANES)
            for zh in range(Z_HI):
                base = zh * CORES * strip
                keep_at = pl.multiple_of(base + mine * strip, 8)
                send_at = pl.multiple_of(base + (1 - mine) * strip, 8)
                kept[tile * Z_HI + zh] = acc[pl.ds(keep_at, strip), lanes]
                sent[tile * Z_HI + zh] = acc[pl.ds(send_at, strip), lanes]


def scaled(x):
    largest = jnp.max(jnp.max(jnp.abs(x), axis=0, keepdims=True), axis=1, keepdims=True)
    exponent = jnp.floor(jnp.log2(jnp.maximum(largest, 2.0**-100))) - 14.0
    return x * jnp.exp2(-exponent), jnp.broadcast_to(exponent, (1, x.shape[1]))


def put_pieces(x, extra, out, rows, step):
    x, exponent = scaled(x)
    extra, extra_exponent = scaled(extra)
    tail = jnp.concatenate([exponent, extra, extra_exponent], axis=0)
    end = rows + tail.shape[0]
    for j in range(x.shape[0] // rows):
        at = j * step
        out[at : at + rows, :] = x[j * rows : (j + 1) * rows, :]
        out[at + rows : at + end, :] = tail
        if end < step:
            out[at + end : at + step, :] = jnp.zeros((step - end, x.shape[1]), F32)


def pack_kernel(rows, step, a, b, extra, out):
    put_pieces(a[...] + b[...], extra[...], out, rows, step)


def unscaled(parts, start, rows):
    return parts[start : start + rows, :] * jnp.exp2(parts[start + rows : start + rows + 1, :])


def sum_kernel(rows, step, parts, extra, out):
    total = unscaled(parts, 0, rows)
    for j in range(1, parts.shape[0] // step):
        total = total + unscaled(parts, j * step, rows)
    put_pieces(total, extra[...], out, rows, step)


def put_product(gram, basis, out):
    half = basis.shape[0]
    rank = basis.shape[1] // Z_HI
    low = jnp.dot(gram[:, :half], basis, precision=HIGHEST, preferred_element_type=F32)
    high = jnp.dot(gram[:, half:], basis, precision=HIGHEST, preferred_element_type=F32)
    product = low[:, :rank] + high[:, rank:]
    strip = product.shape[0] // Z_HI
    packed, exponent = scaled(jnp.concatenate([product[:strip], product[strip:]], axis=1))
    tail = jnp.broadcast_to(exponent, (out.shape[1] - strip, exponent.shape[1]))
    for j in range(out.shape[0]):
        out[j, 0:strip, :] = packed
        out[j, strip:, :] = tail


def take_product(parts, packed):
    count = packed.shape[0]
    peers = N_X * CORES
    strip, step = count // peers, parts.shape[0] // peers
    for j in range(peers):
        packed[j * strip : (j + 1) * strip, :] = unscaled(parts, j * step, strip)


def first_kernel(rows, step, out_pieces, back_pieces, gram, out, flat, basis):
    count = back_pieces.shape[0] // step
    for j in range(count):
        flat[j * rows : (j + 1) * rows, :] = unscaled(back_pieces, j * step, rows)
    mine, total = gram.shape
    for t in range(total // LANES):
        gram[:, t * LANES : (t + 1) * LANES] = flat[t * mine : (t + 1) * mine, :]
    rank = basis.shape[1] // Z_HI
    strip = total // (N_X * Z_HI * CORES)
    share = strip // (4 * Z_HI)
    for j in range(count):
        zh, frm = divmod(j, count // Z_HI)
        place, odd = divmod(frm, 2)
        x, side, c = place // (Z_HI * CORES), place // CORES % Z_HI, place % CORES
        start = (x * CORES + c) * strip + (2 * odd + zh) * (2 * share)
        block = jnp.concatenate(
            [unscaled(p, j * step + rows + 1, share // 2) for p in (out_pieces, back_pieces)], axis=0
        )
        for part in range(2):
            basis[start + part * share : start + (part + 1) * share, side * rank : (side + 1) * rank] = (
                block[:, part * rank : (part + 1) * rank]
            )
    put_product(gram[...], basis[...], out)


def inverse_factor(small):
    n = small.shape[0]
    group = 8
    row_id = lax.broadcasted_iota(jnp.int32, (n, n), 0)
    col_id = lax.broadcasted_iota(jnp.int32, (n, n), 1)
    whole = jnp.concatenate([small, (row_id == col_id).astype(F32)], axis=1)
    blocks = [whole[g * group : (g + 1) * group] for g in range(n // group)]
    sub = lax.broadcasted_iota(jnp.int32, (group, 1), 0)
    done = []
    for k in range(0, n, PIVOTS):
        g, i = divmod(k, group)
        live = blocks[g:]
        cols = [
            [jnp.broadcast_to(b[:, k + m : k + m + 1], b.shape) for b in live] for m in range(PIVOTS)
        ]
        rows = [blocks[g][i + m : i + m + 1, :] for m in range(PIVOTS)]
        corner = [[cols[m][0][i + r : i + r + 1, :] for m in range(PIVOTS)] for r in range(PIVOTS)]
        for m in range(PIVOTS):
            inverse = 1.0 / corner[m][m]
            cols[m] = [c * inverse for c in cols[m]]
            for r in range(m + 1, PIVOTS):
                factor = corner[r][m] * inverse
                rows[r] = rows[r] - factor * rows[m]
                for q in range(m + 1, PIVOTS):
                    corner[r][q] = corner[r][q] - factor * corner[m][q]
                cols[r] = [c - w * corner[m][r] for c, w in zip(cols[r], cols[m])]
            done.append(rows[m] * lax.rsqrt(corner[m][m]))
        for at, block in enumerate(live):
            new = block
            for m in range(PIVOTS):
                new = new - cols[m][at] * rows[m]
            if at == 0:
                new = jnp.where(sub >= i + PIVOTS, new, block)
            blocks[g + at] = new
    return jnp.concatenate(done, axis=0)[:, n:]


def factor_of(packed):
    both = lax.dot_general(
        packed, packed, (((0,), (0,)), ((), ())), precision=HIGHEST, preferred_element_type=F32
    )
    rank = both.shape[0] // Z_HI
    inverse = inverse_factor(both[:rank, :rank] + both[rank:, rank:])
    zero = jnp.zeros_like(inverse)
    return jnp.concatenate(
        [jnp.concatenate([inverse, zero], axis=1), jnp.concatenate([zero, inverse], axis=1)], axis=0
    )


def apply_factor(rows, inverse):
    return lax.dot_general(
        rows, inverse, (((1,), (1,)), ((), ())), precision=HIGHEST, preferred_element_type=F32
    )


def step_kernel(parts, gram, out, packed):
    take_product(parts, packed)
    product = packed[...]
    basis = apply_factor(product, factor_of(product))
    put_product(gram[...], basis, out)


def last_kernel(at, parts, out, packed):
    take_product(parts, packed)
    frames, rank = out.shape
    inverse = factor_of(packed[...])
    rows = packed[pl.ds(pl.multiple_of(at[3], 8), frames), :]
    rows = apply_factor(rows, inverse) * math.sqrt(Z_HI * packed.shape[0])
    out[...] = jnp.where(at[2] == 0, rows[:, :rank], rows[:, rank:])


def call(kernel, outs, ins, args, scratch=()):
    return pl.pallas_call(
        kernel,
        out_shape=outs,
        in_specs=ins,
        out_specs=jax.tree.map(lambda _: VMEM, outs),
        scratch_shapes=list(scratch),
        compiler_params=PARAMS,
    )(*args)


def trade(x, count, axes):
    blocks = lax.all_to_all(x.reshape(count, -1, LANES), axes, 0, 0, tiled=True)
    return blocks.reshape(-1, LANES).astype(F32)


def shift(x, by):
    return lax.ppermute(x, "x", [(i, (i + by) % N_X) for i in range(N_X)])


def swap(x, axis):
    return lax.ppermute(x, axis, [(0, 1), (1, 0)])


def ring_sum(mid, at):
    frames, rank, cols = mid.shape
    piece = shape(frames // 2, rank // N_X, cols, dtype=mid.dtype)
    ends = list(call(pick_kernel, [piece, piece], [SMEM, VMEM], (at, mid)))
    ways = ((1, 0), (-1, frames // 2))
    for step in range(2, N_X + 1):
        for i, (way, first) in enumerate(ways):

            def kernel(at, came, mid, out, way=way, first=first, step=step):
                ring_block(at, mid, step, way, first, out, came)

            ends[i] = call(kernel, piece, [SMEM, VMEM, VMEM], (at, shift(ends[i], way), mid))
    return jnp.concatenate(ends, axis=0)


def local(video, height_factor, width_factor, start_basis):
    rank_h = height_factor.shape[1]
    rank_w = width_factor.shape[1]
    rank_f = start_basis.shape[1]
    frames_dev, _, cols = video.shape
    frm = lax.axis_index(FRM)
    total = frames_dev * lax.axis_size(FRM)
    x_at, zh_at, core_at = lax.axis_index("x"), lax.axis_index("zh"), lax.axis_index("c")
    strip = total // (N_X * Z_HI * CORES)
    frame = frm * frames_dev
    frame_zh = frame // (CORES * strip) % Z_HI
    frame_row = (frame // (Z_HI * CORES * strip) * CORES + frame // strip % CORES) * strip + frame % strip
    at = jnp.stack([x_at, core_at, frame_zh, frame_row, zh_at]).astype(jnp.int32)

    mid = jnp.einsum(
        "fhw,hr->frw", video, height_factor, preferred_element_type=F32
    ).astype(jnp.bfloat16)
    mid = ring_sum(mid, at).transpose(1, 0, 2)

    mid, width = lax.optimization_barrier((mid, width_factor))
    width_other = swap(width, "zh")
    mid = lax.all_to_all(mid, PLANE, 0, 0, tiled=True).reshape(Z_HI, total, cols)
    half = rank_w // CORES
    own, sent = call(
        core_kernel,
        [shape(total, half, dtype=mid.dtype)] * 2,
        [SMEM] + [VMEM] * 3,
        (at, mid, width, width_other),
    )

    core = call(
        add_kernel, shape(total, half, dtype=mid.dtype), [VMEM] * 2, (own, swap(sent, "c"))
    )

    left, right = shift(core, 1), shift(core, -1)
    passed = call(pass_kernel, shape(total, half, dtype=mid.dtype), [SMEM, VMEM, VMEM], (at, left, right))
    ways = [(x * CORES + c, (x + 1 - 2 * c) % N_X * CORES + c) for x in range(N_X) for c in range(CORES)]
    far = lax.ppermute(passed, ("x", "c"), ways)
    mine = Z_HI * strip
    tiles = total // LANES
    kept, sent = call(
        lambda *refs: gram_kernel(1.0 / (rank_h * rank_w), *refs),
        [shape(tiles * Z_HI, strip, LANES)] * 2,
        [SMEM] + [VMEM] * 4,
        (at, core, left, right, far),
        [
            pltpu.VMEM((total, N_X * half), jnp.bfloat16),
            pltpu.VMEM((total // N_X, 2 * LANES), F32),
        ],
    )
    came = swap(sent, "c")

    flat = shape(tiles * mine, LANES)
    count = lax.axis_size(PLANE)
    rows = flat.shape[0] // count
    step = -(-(rows + 2 + frames_dev // (4 * Z_HI)) // 16) * 16
    share = frames_dev // (2 * Z_HI)
    start = lax.dynamic_slice_in_dim(start_basis, zh_at * 2 * share, 2 * share, 0)
    start = jnp.concatenate([start[:share], start[share:]], axis=1)
    upper, lower = start[: share // 2], start[share // 2 :]
    out_pieces = call(
        lambda *refs: pack_kernel(rows, step, *refs),
        shape(count * step, LANES),
        [VMEM] * 3,
        (kept.reshape(flat.shape), came.reshape(flat.shape), upper),
    )
    out_pieces = trade(out_pieces.astype(jnp.float16), count, PLANE)
    piece = call(
        lambda *refs: sum_kernel(rows, step, *refs),
        shape(step, LANES),
        [VMEM] * 2,
        (out_pieces, lower),
    )
    piece = piece.astype(jnp.float16)
    pieces = trade(jnp.broadcast_to(piece[None], (count,) + piece.shape), count, PLANE)

    packed_shape = shape(N_X * CORES, strip + 8, Z_HI * rank_f)
    packed_rows = pltpu.VMEM((total // Z_HI, Z_HI * rank_f), F32)
    gram, packed = call(
        lambda *refs: first_kernel(rows, step, *refs),
        [shape(mine, total), packed_shape],
        [VMEM] * 2,
        (out_pieces, pieces),
        [pltpu.VMEM(flat.shape, F32), packed_rows],
    )
    for step in range(ITERS):
        packed = packed.reshape(-1, packed.shape[2]).astype(jnp.float16)
        packed = trade(packed, N_X * CORES, ("x", "c"))
        if step < ITERS - 1:
            packed = call(step_kernel, packed_shape, [VMEM] * 2, (packed, gram), [packed_rows])
    factor = call(
        last_kernel, shape(frames_dev, rank_f), [SMEM, VMEM], (at, packed), [packed_rows]
    )
    strip_rows = lax.dynamic_slice_in_dim(gram, zh_at * strip, strip, 0)
    column = frame_zh * (total // Z_HI) + frame_row
    gram_out = lax.dynamic_slice_in_dim(strip_rows.T, column, frames_dev, 0)
    return (gram_out, factor)


def solution(mesh):
    frm, hgt, _ = mesh.devices.shape
    fine = Mesh(
        mesh.devices.reshape(frm // Z_LO, Z_LO, hgt, Z_HI, CORES), ("y", "zl", "x", "zh", "c")
    )
    frm, hgt, wid = ("y", "zl"), "x", ("zh", "c")
    return jax.shard_map(
        local,
        mesh=fine,
        in_specs=(P(frm, hgt, wid), P(hgt, None), P(wid, None), P(frm, None)),
        out_specs=(P(frm, ("x", "zh", "c")), P(frm, None)),
        check_vma=False,
    )
```

```python
import math

import jax
import jax.numpy as jnp
from jax import lax
from jax.experimental import pallas as pl
from jax.experimental.pallas import tpu as pltpu
from jax.sharding import Mesh, PartitionSpec as P

ITERS = 3
Z_HI = 2
CORES = 2
Z_LO = 4
N_X = 4
LANES = 128
FRM = ("y", "zl")
PLANE = ("zh", "y", "zl")
PIVOTS = 8
VMEM = pl.BlockSpec(memory_space=pltpu.VMEM)
SMEM = pl.BlockSpec(memory_space=pltpu.SMEM)
PARAMS = pltpu.CompilerParams(vmem_limit_bytes=40 << 20)
F32 = jnp.float32
HIGHEST = lax.Precision.HIGHEST


def shape(*dims, dtype=F32):
    return jax.ShapeDtypeStruct(dims, dtype)


def pick_kernel(at, mid, out_a, out_b):
    for way, first, out in ((1, 0, out_a), (-1, mid.shape[0] // 2, out_b)):
        ring_block(at, mid, 1, way, first, out, None)


def ring_block(at, mid, step, way, first, out, came):
    half, block, _ = out.shape
    start = pl.multiple_of(lax.rem(at[0] - way * step + 2 * N_X, N_X) * block, 64)
    for f in range(half):
        own = mid[first + f, pl.ds(start, block), :]
        if came is not None:
            own = (own.astype(F32) + came[f].astype(F32)).astype(out.dtype)
        out[f] = own


def copies_kernel(a, b, out):
    total = (a[...].astype(F32) + b[...].astype(F32)).astype(out.dtype)
    for j in range(out.shape[0]):
        out[j] = total


def core_kernel(at, mid, width, width_other, own, sent):
    half = own.shape[1]
    zh = at[4]
    part = jnp.dot(mid[zh], width[...], preferred_element_type=F32) + jnp.dot(
        mid[1 - zh], width_other[...], preferred_element_type=F32
    )
    low, high = part[:, :half].astype(own.dtype), part[:, half:].astype(own.dtype)
    first = at[1] == 0

    @pl.when(first)
    def _():
        own[...] = low
        sent[...] = high

    @pl.when(jnp.logical_not(first))
    def _():
        own[...] = high
        sent[...] = low


def gram_kernel(scale, at, blocks, kept, sent, core, acc):
    _, total, depth = blocks.shape
    strip = kept.shape[1]
    for j in range(N_X):
        for x in range(N_X):
            for zh in range(Z_HI):
                for c in range(CORES):
                    source = ((x * Z_HI + zh) * CORES + c) * strip
                    place = ((zh * N_X + x) * CORES + c) * strip
                    core[place : place + strip, j * depth : (j + 1) * depth] = blocks[
                        j, source : source + strip, :
                    ]
    rows = []
    for zh in range(Z_HI):
        start = zh * (total // Z_HI) + at[0] * (CORES * strip)
        rows.append(core[pl.ds(pl.multiple_of(start, 32), CORES * strip), :])
    rows = jnp.concatenate(rows, axis=0)
    mine = at[1]
    wide = 2 * LANES
    for pair in range(total // wide):
        acc[...] = scale * lax.dot_general(
            rows,
            core[pair * wide : (pair + 1) * wide, :],
            (((1,), (1,)), ((), ())),
            preferred_element_type=F32,
        )
        for side in range(2):
            tile = 2 * pair + side
            lanes = slice(side * LANES, (side + 1) * LANES)
            for zh in range(Z_HI):
                base = zh * CORES * strip
                keep_at = pl.multiple_of(base + mine * strip, 8)
                send_at = pl.multiple_of(base + (1 - mine) * strip, 8)
                kept[tile * Z_HI + zh] = acc[pl.ds(keep_at, strip), lanes]
                sent[tile * Z_HI + zh] = acc[pl.ds(send_at, strip), lanes]


def scaled(x):
    largest = jnp.max(jnp.max(jnp.abs(x), axis=0, keepdims=True), axis=1, keepdims=True)
    exponent = jnp.floor(jnp.log2(jnp.maximum(largest, 2.0**-100))) - 14.0
    return x * jnp.exp2(-exponent), jnp.broadcast_to(exponent, (1, x.shape[1]))


def put_pieces(x, extra, out, rows, step):
    x, exponent = scaled(x)
    extra, extra_exponent = scaled(extra)
    tail = jnp.concatenate([exponent, extra, extra_exponent], axis=0)
    end = rows + tail.shape[0]
    for j in range(x.shape[0] // rows):
        at = j * step
        out[at : at + rows, :] = x[j * rows : (j + 1) * rows, :]
        out[at + rows : at + end, :] = tail
        if end < step:
            out[at + end : at + step, :] = jnp.zeros((step - end, x.shape[1]), F32)


def pack_kernel(rows, step, a, b, extra, out):
    put_pieces(a[...] + b[...], extra[...], out, rows, step)


def unscaled(parts, start, rows):
    return parts[start : start + rows, :] * jnp.exp2(parts[start + rows : start + rows + 1, :])


def sum_kernel(rows, step, parts, extra, out):
    total = unscaled(parts, 0, rows)
    for j in range(1, parts.shape[0] // step):
        total = total + unscaled(parts, j * step, rows)
    put_pieces(total, extra[...], out, rows, step)


def put_product(gram, basis, out):
    half = basis.shape[0]
    rank = basis.shape[1] // Z_HI
    low = jnp.dot(gram[:, :half], basis, precision=HIGHEST, preferred_element_type=F32)
    high = jnp.dot(gram[:, half:], basis, precision=HIGHEST, preferred_element_type=F32)
    product = low[:, :rank] + high[:, rank:]
    strip = product.shape[0] // Z_HI
    packed, exponent = scaled(jnp.concatenate([product[:strip], product[strip:]], axis=1))
    tail = jnp.broadcast_to(exponent, (out.shape[1] - strip, exponent.shape[1]))
    for j in range(out.shape[0]):
        out[j, 0:strip, :] = packed
        out[j, strip:, :] = tail


def take_product(parts, packed):
    count = packed.shape[0]
    peers = N_X * CORES
    strip, step = count // peers, parts.shape[0] // peers
    for j in range(peers):
        packed[j * strip : (j + 1) * strip, :] = unscaled(parts, j * step, strip)


def first_kernel(rows, step, out_pieces, back_pieces, gram, out, flat, basis):
    count = back_pieces.shape[0] // step
    for j in range(count):
        flat[j * rows : (j + 1) * rows, :] = unscaled(back_pieces, j * step, rows)
    mine, total = gram.shape
    for t in range(total // LANES):
        gram[:, t * LANES : (t + 1) * LANES] = flat[t * mine : (t + 1) * mine, :]
    rank = basis.shape[1] // Z_HI
    strip = total // (N_X * Z_HI * CORES)
    share = strip // (4 * Z_HI)
    for j in range(count):
        zh, frm = divmod(j, count // Z_HI)
        place, odd = divmod(frm, 2)
        x, side, c = place // (Z_HI * CORES), place // CORES % Z_HI, place % CORES
        start = (x * CORES + c) * strip + (2 * odd + zh) * (2 * share)
        block = jnp.concatenate(
            [unscaled(p, j * step + rows + 1, share // 2) for p in (out_pieces, back_pieces)], axis=0
        )
        for part in range(2):
            basis[start + part * share : start + (part + 1) * share, side * rank : (side + 1) * rank] = (
                block[:, part * rank : (part + 1) * rank]
            )
    put_product(gram[...], basis[...], out)


def inverse_factor(small):
    n = small.shape[0]
    group = 8
    row_id = lax.broadcasted_iota(jnp.int32, (n, n), 0)
    col_id = lax.broadcasted_iota(jnp.int32, (n, n), 1)
    whole = jnp.concatenate([small, (row_id == col_id).astype(F32)], axis=1)
    blocks = [whole[g * group : (g + 1) * group] for g in range(n // group)]
    sub = lax.broadcasted_iota(jnp.int32, (group, 1), 0)
    done = []
    for k in range(0, n, PIVOTS):
        g, i = divmod(k, group)
        live = blocks[g:]
        cols = [
            [jnp.broadcast_to(b[:, k + m : k + m + 1], b.shape) for b in live] for m in range(PIVOTS)
        ]
        rows = [blocks[g][i + m : i + m + 1, :] for m in range(PIVOTS)]
        corner = [[cols[m][0][i + r : i + r + 1, :] for m in range(PIVOTS)] for r in range(PIVOTS)]
        for m in range(PIVOTS):
            inverse = 1.0 / corner[m][m]
            cols[m] = [c * inverse for c in cols[m]]
            for r in range(m + 1, PIVOTS):
                factor = corner[r][m] * inverse
                rows[r] = rows[r] - factor * rows[m]
                for q in range(m + 1, PIVOTS):
                    corner[r][q] = corner[r][q] - factor * corner[m][q]
                cols[r] = [c - w * corner[m][r] for c, w in zip(cols[r], cols[m])]
            done.append(rows[m] * lax.rsqrt(corner[m][m]))
        for at, block in enumerate(live):
            new = block
            for m in range(PIVOTS):
                new = new - cols[m][at] * rows[m]
            if at == 0:
                new = jnp.where(sub >= i + PIVOTS, new, block)
            blocks[g + at] = new
    return jnp.concatenate(done, axis=0)[:, n:]


def factor_of(packed):
    both = lax.dot_general(
        packed, packed, (((0,), (0,)), ((), ())), precision=HIGHEST, preferred_element_type=F32
    )
    rank = both.shape[0] // Z_HI
    inverse = inverse_factor(both[:rank, :rank] + both[rank:, rank:])
    zero = jnp.zeros_like(inverse)
    return jnp.concatenate(
        [jnp.concatenate([inverse, zero], axis=1), jnp.concatenate([zero, inverse], axis=1)], axis=0
    )


def apply_factor(rows, inverse):
    return lax.dot_general(
        rows, inverse, (((1,), (1,)), ((), ())), precision=HIGHEST, preferred_element_type=F32
    )


def step_kernel(parts, gram, out, packed):
    take_product(parts, packed)
    product = packed[...]
    basis = apply_factor(product, factor_of(product))
    put_product(gram[...], basis, out)


def last_kernel(at, parts, out, packed):
    take_product(parts, packed)
    frames, rank = out.shape
    inverse = factor_of(packed[...])
    rows = packed[pl.ds(pl.multiple_of(at[3], 8), frames), :]
    rows = apply_factor(rows, inverse) * math.sqrt(Z_HI * packed.shape[0])
    out[...] = jnp.where(at[2] == 0, rows[:, :rank], rows[:, rank:])


def call(kernel, outs, ins, args, scratch=()):
    return pl.pallas_call(
        kernel,
        out_shape=outs,
        in_specs=ins,
        out_specs=jax.tree.map(lambda _: VMEM, outs),
        scratch_shapes=list(scratch),
        compiler_params=PARAMS,
    )(*args)


def trade(x, count, axes):
    blocks = lax.all_to_all(x.reshape(count, -1, LANES), axes, 0, 0, tiled=True)
    return blocks.reshape(-1, LANES).astype(F32)


def shift(x, by):
    return lax.ppermute(x, "x", [(i, (i + by) % N_X) for i in range(N_X)])


def swap(x, axis):
    return lax.ppermute(x, axis, [(0, 1), (1, 0)])


def ring_sum(mid, at):
    frames, rank, cols = mid.shape
    piece = shape(frames // 2, rank // N_X, cols, dtype=mid.dtype)
    ends = list(call(pick_kernel, [piece, piece], [SMEM, VMEM], (at, mid)))
    ways = ((1, 0), (-1, frames // 2))
    for step in range(2, N_X + 1):
        for i, (way, first) in enumerate(ways):

            def kernel(at, came, mid, out, way=way, first=first, step=step):
                ring_block(at, mid, step, way, first, out, came)

            ends[i] = call(kernel, piece, [SMEM, VMEM, VMEM], (at, shift(ends[i], way), mid))
    return jnp.concatenate(ends, axis=0)


def local(video, height_factor, width_factor, start_basis):
    rank_h = height_factor.shape[1]
    rank_w = width_factor.shape[1]
    rank_f = start_basis.shape[1]
    frames_dev, _, cols = video.shape
    frm = lax.axis_index(FRM)
    total = frames_dev * lax.axis_size(FRM)
    x_at, zh_at, core_at = lax.axis_index("x"), lax.axis_index("zh"), lax.axis_index("c")
    strip = total // (N_X * Z_HI * CORES)
    frame = frm * frames_dev
    frame_zh = frame // (CORES * strip) % Z_HI
    frame_row = (frame // (Z_HI * CORES * strip) * CORES + frame // strip % CORES) * strip + frame % strip
    at = jnp.stack([x_at, core_at, frame_zh, frame_row, zh_at]).astype(jnp.int32)

    mid = jnp.einsum(
        "fhw,hr->frw", video, height_factor, preferred_element_type=F32
    ).astype(jnp.bfloat16)
    mid = ring_sum(mid, at).transpose(1, 0, 2)

    mid, width = lax.optimization_barrier((mid, width_factor))
    width_other = swap(width, "zh")
    mid = lax.all_to_all(mid, PLANE, 0, 0, tiled=True).reshape(Z_HI, total, cols)
    half = rank_w // CORES
    own, sent = call(
        core_kernel,
        [shape(total, half, dtype=mid.dtype)] * 2,
        [SMEM] + [VMEM] * 3,
        (at, mid, width, width_other),
    )


    copies = call(
        copies_kernel, shape(N_X, total, half, dtype=mid.dtype), [VMEM] * 2, (own, swap(sent, "c"))
    )
    blocks = lax.all_to_all(copies, "x", 0, 0, tiled=True)
    mine = Z_HI * strip
    tiles = total // LANES
    kept, sent = call(
        lambda *refs: gram_kernel(1.0 / (rank_h * rank_w), *refs),
        [shape(tiles * Z_HI, strip, LANES)] * 2,
        [SMEM, VMEM],
        (at, blocks),
        [
            pltpu.VMEM((total, N_X * half), jnp.bfloat16),
            pltpu.VMEM((total // N_X, 2 * LANES), F32),
        ],
    )
    came = swap(sent, "c")

    flat = shape(tiles * mine, LANES)
    count = lax.axis_size(PLANE)
    rows = flat.shape[0] // count
    step = -(-(rows + 2 + frames_dev // (4 * Z_HI)) // 16) * 16
    share = frames_dev // (2 * Z_HI)
    start = lax.dynamic_slice_in_dim(start_basis, zh_at * 2 * share, 2 * share, 0)
    start = jnp.concatenate([start[:share], start[share:]], axis=1)
    upper, lower = start[: share // 2], start[share // 2 :]
    out_pieces = call(
        lambda *refs: pack_kernel(rows, step, *refs),
        shape(count * step, LANES),
        [VMEM] * 3,
        (kept.reshape(flat.shape), came.reshape(flat.shape), upper),
    )
    out_pieces = trade(out_pieces.astype(jnp.float16), count, PLANE)
    piece = call(
        lambda *refs: sum_kernel(rows, step, *refs),
        shape(step, LANES),
        [VMEM] * 2,
        (out_pieces, lower),
    )
    piece = piece.astype(jnp.float16)
    pieces = trade(jnp.broadcast_to(piece[None], (count,) + piece.shape), count, PLANE)

    packed_shape = shape(N_X * CORES, strip + 8, Z_HI * rank_f)
    packed_rows = pltpu.VMEM((total // Z_HI, Z_HI * rank_f), F32)
    gram, packed = call(
        lambda *refs: first_kernel(rows, step, *refs),
        [shape(mine, total), packed_shape],
        [VMEM] * 2,
        (out_pieces, pieces),
        [pltpu.VMEM(flat.shape, F32), packed_rows],
    )
    for step in range(ITERS):
        packed = packed.reshape(-1, packed.shape[2]).astype(jnp.float16)
        packed = trade(packed, N_X * CORES, ("x", "c"))
        if step < ITERS - 1:
            packed = call(step_kernel, packed_shape, [VMEM] * 2, (packed, gram), [packed_rows])
    factor = call(
        last_kernel, shape(frames_dev, rank_f), [SMEM, VMEM], (at, packed), [packed_rows]
    )
    strip_rows = lax.dynamic_slice_in_dim(gram, zh_at * strip, strip, 0)
    column = frame_zh * (total // Z_HI) + frame_row
    gram_out = lax.dynamic_slice_in_dim(strip_rows.T, column, frames_dev, 0)
    return (gram_out, factor)


def solution(mesh):
    frm, hgt, _ = mesh.devices.shape
    fine = Mesh(
        mesh.devices.reshape(frm // Z_LO, Z_LO, hgt, Z_HI, CORES), ("y", "zl", "x", "zh", "c")
    )
    frm, hgt, wid = ("y", "zl"), "x", ("zh", "c")
    return jax.shard_map(
        local,
        mesh=fine,
        in_specs=(P(frm, hgt, wid), P(hgt, None), P(wid, None), P(frm, None)),
        out_specs=(P(frm, ("x", "zh", "c")), P(frm, None)),
        check_vma=False,
    )
```

```python
import math

import jax
import jax.numpy as jnp
from jax import lax
from jax.experimental import pallas as pl
from jax.experimental.pallas import tpu as pltpu
from jax.sharding import Mesh, PartitionSpec as P

ITERS = 3
Z_HI = 2
CORES = 2
Z_LO = 4
N_X = 4
LANES = 128
FRM = ("y", "zl")
PLANE = ("zh", "y", "zl")
PIVOTS = 8
VMEM = pl.BlockSpec(memory_space=pltpu.VMEM)
SMEM = pl.BlockSpec(memory_space=pltpu.SMEM)
PARAMS = pltpu.CompilerParams(vmem_limit_bytes=40 << 20)
F32 = jnp.float32
HIGHEST = lax.Precision.HIGHEST


def shape(*dims, dtype=F32):
    return jax.ShapeDtypeStruct(dims, dtype)


def pick_kernel(at, mid, out_a, out_b):
    for way, first, out in ((1, 0, out_a), (-1, mid.shape[0] // 2, out_b)):
        ring_block(at, mid, 1, way, first, out, None)


def ring_block(at, mid, step, way, first, out, came):
    half, block, _ = out.shape
    start = pl.multiple_of(lax.rem(at[0] - way * step + 2 * N_X, N_X) * block, 64)
    for f in range(half):
        own = mid[first + f, pl.ds(start, block), :]
        if came is not None:
            own = (own.astype(F32) + came[f].astype(F32)).astype(out.dtype)
        out[f] = own


def copies_kernel(a, b, out):
    total = (a[...].astype(F32) + b[...].astype(F32)).astype(out.dtype)
    for j in range(out.shape[0]):
        out[j] = total


def core_kernel(at, mid, width, width_other, own, sent):
    half = own.shape[1]
    zh = at[4]
    part = jnp.dot(mid[zh], width[...], preferred_element_type=F32) + jnp.dot(
        mid[1 - zh], width_other[...], preferred_element_type=F32
    )
    low, high = part[:, :half].astype(own.dtype), part[:, half:].astype(own.dtype)
    first = at[1] == 0

    @pl.when(first)
    def _():
        own[...] = low
        sent[...] = high

    @pl.when(jnp.logical_not(first))
    def _():
        own[...] = high
        sent[...] = low


def gram_kernel(scale, at, blocks, kept, sent, core, acc):
    _, total, depth = blocks.shape
    strip = kept.shape[1]
    for j in range(N_X):
        for x in range(N_X):
            for zh in range(Z_HI):
                for c in range(CORES):
                    source = ((x * Z_HI + zh) * CORES + c) * strip
                    place = ((zh * N_X + x) * CORES + c) * strip
                    core[place : place + strip, j * depth : (j + 1) * depth] = blocks[
                        j, source : source + strip, :
                    ]
    rows = []
    for zh in range(Z_HI):
        start = zh * (total // Z_HI) + at[0] * (CORES * strip)
        rows.append(core[pl.ds(pl.multiple_of(start, 32), CORES * strip), :])
    rows = jnp.concatenate(rows, axis=0)
    mine = at[1]
    wide = 2 * LANES
    for pair in range(total // wide):
        acc[...] = scale * lax.dot_general(
            rows,
            core[pair * wide : (pair + 1) * wide, :],
            (((1,), (1,)), ((), ())),
            preferred_element_type=F32,
        )
        for side in range(2):
            tile = 2 * pair + side
            lanes = slice(side * LANES, (side + 1) * LANES)
            for zh in range(Z_HI):
                base = zh * CORES * strip
                keep_at = pl.multiple_of(base + mine * strip, 8)
                send_at = pl.multiple_of(base + (1 - mine) * strip, 8)
                kept[tile * Z_HI + zh] = acc[pl.ds(keep_at, strip), lanes]
                sent[tile * Z_HI + zh] = acc[pl.ds(send_at, strip), lanes]


def scaled(x):
    largest = jnp.max(jnp.max(jnp.abs(x), axis=0, keepdims=True), axis=1, keepdims=True)
    exponent = jnp.floor(jnp.log2(jnp.maximum(largest, 2.0**-100))) - 14.0
    return x * jnp.exp2(-exponent), jnp.broadcast_to(exponent, (1, x.shape[1]))


def put_pieces(x, extra, out, rows, step):
    x, exponent = scaled(x)
    extra, extra_exponent = scaled(extra)
    tail = jnp.concatenate([exponent, extra, extra_exponent], axis=0)
    end = rows + tail.shape[0]
    for j in range(x.shape[0] // rows):
        at = j * step
        out[at : at + rows, :] = x[j * rows : (j + 1) * rows, :]
        out[at + rows : at + end, :] = tail
        if end < step:
            out[at + end : at + step, :] = jnp.zeros((step - end, x.shape[1]), F32)


def pack_kernel(rows, step, a, b, extra, out):
    put_pieces(a[...] + b[...], extra[...], out, rows, step)


def unscaled(parts, start, rows):
    return parts[start : start + rows, :] * jnp.exp2(parts[start + rows : start + rows + 1, :])


def sum_kernel(rows, step, parts, extra, out):
    total = unscaled(parts, 0, rows)
    for j in range(1, parts.shape[0] // step):
        total = total + unscaled(parts, j * step, rows)
    put_pieces(total, extra[...], out, rows, step)


def halves(x):
    upper = x.astype(jnp.bfloat16)
    return upper, (x - upper.astype(F32)).astype(jnp.bfloat16)


def split_dot(a, b, dims):
    a_upper, a_lower = halves(a)
    b_upper, b_lower = halves(b)
    both = jnp.concatenate([b_upper, b_lower], axis=1 - dims[1])
    wide = lax.dot_general(
        a_upper, both, (((dims[0],), (dims[1],)), ((), ())), preferred_element_type=F32
    )
    count = wide.shape[1] // 2
    return wide[:, :count] + wide[:, count:] + lax.dot_general(
        a_lower, b_upper, (((dims[0],), (dims[1],)), ((), ())), preferred_element_type=F32
    )


def put_product(gram, basis, out):
    half = basis.shape[0]
    rank = basis.shape[1] // Z_HI
    low = split_dot(gram[:, :half], basis, (1, 0))
    high = split_dot(gram[:, half:], basis, (1, 0))
    product = low[:, :rank] + high[:, rank:]
    strip = product.shape[0] // Z_HI
    packed, exponent = scaled(jnp.concatenate([product[:strip], product[strip:]], axis=1))
    tail = jnp.broadcast_to(exponent, (out.shape[1] - strip, exponent.shape[1]))
    for j in range(out.shape[0]):
        out[j, 0:strip, :] = packed
        out[j, strip:, :] = tail


def take_product(parts, packed):
    count = packed.shape[0]
    peers = N_X * CORES
    strip, step = count // peers, parts.shape[0] // peers
    for j in range(peers):
        packed[j * strip : (j + 1) * strip, :] = unscaled(parts, j * step, strip)


def first_kernel(rows, step, out_pieces, back_pieces, gram, out, flat, basis):
    count = back_pieces.shape[0] // step
    for j in range(count):
        flat[j * rows : (j + 1) * rows, :] = unscaled(back_pieces, j * step, rows)
    mine, total = gram.shape
    for t in range(total // LANES):
        gram[:, t * LANES : (t + 1) * LANES] = flat[t * mine : (t + 1) * mine, :]
    rank = basis.shape[1] // Z_HI
    strip = total // (N_X * Z_HI * CORES)
    share = strip // (4 * Z_HI)
    for j in range(count):
        zh, frm = divmod(j, count // Z_HI)
        place, odd = divmod(frm, 2)
        x, side, c = place // (Z_HI * CORES), place // CORES % Z_HI, place % CORES
        start = (x * CORES + c) * strip + (2 * odd + zh) * (2 * share)
        block = jnp.concatenate(
            [unscaled(p, j * step + rows + 1, share // 2) for p in (out_pieces, back_pieces)], axis=0
        )
        for part in range(2):
            basis[start + part * share : start + (part + 1) * share, side * rank : (side + 1) * rank] = (
                block[:, part * rank : (part + 1) * rank]
            )
    put_product(gram[...], basis[...], out)


def inverse_factor(small):
    n = small.shape[0]
    group = 8
    row_id = lax.broadcasted_iota(jnp.int32, (n, n), 0)
    col_id = lax.broadcasted_iota(jnp.int32, (n, n), 1)
    whole = jnp.concatenate([small, (row_id == col_id).astype(F32)], axis=1)
    blocks = [whole[g * group : (g + 1) * group] for g in range(n // group)]
    sub = lax.broadcasted_iota(jnp.int32, (group, 1), 0)
    done = []
    for k in range(0, n, PIVOTS):
        g, i = divmod(k, group)
        live = blocks[g:]
        cols = [
            [jnp.broadcast_to(b[:, k + m : k + m + 1], b.shape) for b in live] for m in range(PIVOTS)
        ]
        rows = [blocks[g][i + m : i + m + 1, :] for m in range(PIVOTS)]
        corner = [[cols[m][0][i + r : i + r + 1, :] for m in range(PIVOTS)] for r in range(PIVOTS)]
        for m in range(PIVOTS):
            inverse = 1.0 / corner[m][m]
            cols[m] = [c * inverse for c in cols[m]]
            for r in range(m + 1, PIVOTS):
                factor = corner[r][m] * inverse
                rows[r] = rows[r] - factor * rows[m]
                for q in range(m + 1, PIVOTS):
                    corner[r][q] = corner[r][q] - factor * corner[m][q]
                cols[r] = [c - w * corner[m][r] for c, w in zip(cols[r], cols[m])]
            done.append(rows[m] * lax.rsqrt(corner[m][m]))
        for at, block in enumerate(live):
            new = block
            for m in range(PIVOTS):
                new = new - cols[m][at] * rows[m]
            if at == 0:
                new = jnp.where(sub >= i + PIVOTS, new, block)
            blocks[g + at] = new
    return jnp.concatenate(done, axis=0)[:, n:]


def factor_of(packed):
    parts = jnp.concatenate(halves(packed), axis=1)
    both = lax.dot_general(
        parts, parts, (((0,), (0,)), ((), ())), preferred_element_type=F32
    )
    count = packed.shape[1]
    both = (both[:count, :count] + both[count:, count:]) + (both[:count, count:] + both[count:, :count])
    rank = count // Z_HI
    inverse = inverse_factor(both[:rank, :rank] + both[rank:, rank:])
    zero = jnp.zeros_like(inverse)
    return jnp.concatenate(
        [jnp.concatenate([inverse, zero], axis=1), jnp.concatenate([zero, inverse], axis=1)], axis=0
    )


def apply_factor(rows, inverse):
    return lax.dot_general(
        rows, inverse, (((1,), (1,)), ((), ())), precision=HIGHEST, preferred_element_type=F32
    )


def step_kernel(parts, gram, out, packed):
    take_product(parts, packed)
    product = packed[...]
    basis = split_dot(product, factor_of(product), (1, 1))
    put_product(gram[...], basis, out)


def last_kernel(at, parts, out, packed):
    take_product(parts, packed)
    frames, rank = out.shape
    inverse = factor_of(packed[...])
    rows = packed[pl.ds(pl.multiple_of(at[3], 8), frames), :]
    rows = apply_factor(rows, inverse) * math.sqrt(Z_HI * packed.shape[0])
    out[...] = jnp.where(at[2] == 0, rows[:, :rank], rows[:, rank:])


def call(kernel, outs, ins, args, scratch=()):
    return pl.pallas_call(
        kernel,
        out_shape=outs,
        in_specs=ins,
        out_specs=jax.tree.map(lambda _: VMEM, outs),
        scratch_shapes=list(scratch),
        compiler_params=PARAMS,
    )(*args)


def trade(x, count, axes):
    blocks = lax.all_to_all(x.reshape(count, -1, LANES), axes, 0, 0, tiled=True)
    return blocks.reshape(-1, LANES).astype(F32)


def shift(x, by):
    return lax.ppermute(x, "x", [(i, (i + by) % N_X) for i in range(N_X)])


def swap(x, axis):
    return lax.ppermute(x, axis, [(0, 1), (1, 0)])


def ring_sum(mid, at):
    frames, rank, cols = mid.shape
    piece = shape(frames // 2, rank // N_X, cols, dtype=mid.dtype)
    ends = list(call(pick_kernel, [piece, piece], [SMEM, VMEM], (at, mid)))
    ways = ((1, 0), (-1, frames // 2))
    for step in range(2, N_X + 1):
        for i, (way, first) in enumerate(ways):

            def kernel(at, came, mid, out, way=way, first=first, step=step):
                ring_block(at, mid, step, way, first, out, came)

            ends[i] = call(kernel, piece, [SMEM, VMEM, VMEM], (at, shift(ends[i], way), mid))
    return jnp.concatenate(ends, axis=0)


def local(video, height_factor, width_factor, start_basis):
    rank_h = height_factor.shape[1]
    rank_w = width_factor.shape[1]
    rank_f = start_basis.shape[1]
    frames_dev, _, cols = video.shape
    frm = lax.axis_index(FRM)
    total = frames_dev * lax.axis_size(FRM)
    x_at, zh_at, core_at = lax.axis_index("x"), lax.axis_index("zh"), lax.axis_index("c")
    strip = total // (N_X * Z_HI * CORES)
    frame = frm * frames_dev
    frame_zh = frame // (CORES * strip) % Z_HI
    frame_row = (frame // (Z_HI * CORES * strip) * CORES + frame // strip % CORES) * strip + frame % strip
    at = jnp.stack([x_at, core_at, frame_zh, frame_row, zh_at]).astype(jnp.int32)

    mid = jnp.einsum(
        "fhw,hr->frw", video, height_factor, preferred_element_type=F32
    ).astype(jnp.bfloat16)
    mid = ring_sum(mid, at).transpose(1, 0, 2)

    mid, width = lax.optimization_barrier((mid, width_factor))
    width_other = swap(width, "zh")
    mid = lax.all_to_all(mid, PLANE, 0, 0, tiled=True).reshape(Z_HI, total, cols)
    half = rank_w // CORES
    own, sent = call(
        core_kernel,
        [shape(total, half, dtype=mid.dtype)] * 2,
        [SMEM] + [VMEM] * 3,
        (at, mid, width, width_other),
    )


    copies = call(
        copies_kernel, shape(N_X, total, half, dtype=mid.dtype), [VMEM] * 2, (own, swap(sent, "c"))
    )
    blocks = lax.all_to_all(copies, "x", 0, 0, tiled=True)
    mine = Z_HI * strip
    tiles = total // LANES
    kept, sent = call(
        lambda *refs: gram_kernel(1.0 / (rank_h * rank_w), *refs),
        [shape(tiles * Z_HI, strip, LANES)] * 2,
        [SMEM, VMEM],
        (at, blocks),
        [
            pltpu.VMEM((total, N_X * half), jnp.bfloat16),
            pltpu.VMEM((total // N_X, 2 * LANES), F32),
        ],
    )
    came = swap(sent, "c")

    flat = shape(tiles * mine, LANES)
    count = lax.axis_size(PLANE)
    rows = flat.shape[0] // count
    step = -(-(rows + 2 + frames_dev // (4 * Z_HI)) // 16) * 16
    share = frames_dev // (2 * Z_HI)
    start = lax.dynamic_slice_in_dim(start_basis, zh_at * 2 * share, 2 * share, 0)
    start = jnp.concatenate([start[:share], start[share:]], axis=1)
    upper, lower = start[: share // 2], start[share // 2 :]
    out_pieces = call(
        lambda *refs: pack_kernel(rows, step, *refs),
        shape(count * step, LANES),
        [VMEM] * 3,
        (kept.reshape(flat.shape), came.reshape(flat.shape), upper),
    )
    out_pieces = trade(out_pieces.astype(jnp.float16), count, PLANE)
    piece = call(
        lambda *refs: sum_kernel(rows, step, *refs),
        shape(step, LANES),
        [VMEM] * 2,
        (out_pieces, lower),
    )
    piece = piece.astype(jnp.float16)
    pieces = trade(jnp.broadcast_to(piece[None], (count,) + piece.shape), count, PLANE)

    packed_shape = shape(N_X * CORES, strip + 8, Z_HI * rank_f)
    packed_rows = pltpu.VMEM((total // Z_HI, Z_HI * rank_f), F32)
    gram, packed = call(
        lambda *refs: first_kernel(rows, step, *refs),
        [shape(mine, total), packed_shape],
        [VMEM] * 2,
        (out_pieces, pieces),
        [pltpu.VMEM(flat.shape, F32), packed_rows],
    )
    for step in range(ITERS):
        packed = packed.reshape(-1, packed.shape[2]).astype(jnp.float16)
        packed = trade(packed, N_X * CORES, ("x", "c"))
        if step < ITERS - 1:
            packed = call(step_kernel, packed_shape, [VMEM] * 2, (packed, gram), [packed_rows])
    factor = call(
        last_kernel, shape(frames_dev, rank_f), [SMEM, VMEM], (at, packed), [packed_rows]
    )
    strip_rows = lax.dynamic_slice_in_dim(gram, zh_at * strip, strip, 0)
    column = frame_zh * (total // Z_HI) + frame_row
    gram_out = lax.dynamic_slice_in_dim(strip_rows.T, column, frames_dev, 0)
    return (gram_out, factor)


def solution(mesh):
    frm, hgt, _ = mesh.devices.shape
    fine = Mesh(
        mesh.devices.reshape(frm // Z_LO, Z_LO, hgt, Z_HI, CORES), ("y", "zl", "x", "zh", "c")
    )
    frm, hgt, wid = ("y", "zl"), "x", ("zh", "c")
    return jax.shard_map(
        local,
        mesh=fine,
        in_specs=(P(frm, hgt, wid), P(hgt, None), P(wid, None), P(frm, None)),
        out_specs=(P(frm, ("x", "zh", "c")), P(frm, None)),
        check_vma=False,
    )
```
